32 devices in a mesh: rows: 16 (over z, x, core), inner: 2 (over y).
Axes of the slice: x: 2, y: 2, z: 4, core: 2. Of those that a mesh axis runs over, the one named last changes fastest.
Arguments:
- hardness_blocks: float32 [80, 4, 128, 128], P('rows', None, 'inner'), may hold values from -0.046875 to 0.046875
- inverse_blocks: float32 [80, 6, 128, 128], P('rows', None, 'inner'), may hold values from -6 to 6
- hardness_pattern: int32 [80, 4], P('rows'), may hold values from 0 to 79, as said below
- inverse_pattern: int32 [80, 6], replicated, may hold values from 0 to 79, as said below
Outputs:
- updated_blocks: float32 [80, 6, 128, 128], P('rows', None, 'inner')
The draws below stay inside these ranges and needn't reach their ends.
Inputs may be any that keep to these rules, and one draw needn't show every extreme that they name: `hardness_pattern`: row i lists 4 different block columns, the first being i, all within 5 of i. `inverse_pattern`: row i lists 6 different block columns, the first being i, all within 5 of i.
All inputs are finite; a program needn't handle non-finite values.
Results may differ from the reference program's by a relative error of at most 0.0001.
Values sent between devices are 32-bit elements; how exact they have to be, the bound alone decides.
No kernel may reach another device: no remote copies, remote signals or barrier semaphores. Data moves between devices by JAX's collectives and lax.ppermute only.
A program may use at most 64 MiB of HBM per device.

```python
import jax
import jax.numpy as jnp
from jax import lax

B = 128
KJ = 4
KZ = 6
REACH = 5
NB = 80


def pattern_draw(key, count):
    rows_index = jnp.arange(NB, dtype=jnp.int32)
    scores = jax.random.randint(key, (NB, REACH), 0, 1 << 20) * REACH + jnp.arange(REACH, dtype=jnp.int32)
    order = jnp.argsort(scores, axis=1)
    magnitude = (order[:, :count - 1] + 1).astype(jnp.int32)
    signs = jax.random.randint(jax.random.fold_in(key, 7), (NB, count - 1), 0, 2) * 2 - 1
    column = rows_index[:, None] + signs * magnitude
    outside = (column < 0) | (column >= NB)
    column = jnp.where(outside, rows_index[:, None] - signs * magnitude, column)
    return jnp.concatenate([rows_index[:, None], column], axis=1).astype(jnp.int32)


def draw_hardness_pattern(key, part):
    key = jax.random.fold_in(key, 1)
    return pattern_draw(key, KJ)


def draw_inverse_pattern(key, part):
    key = jax.random.fold_in(key, 2)
    return pattern_draw(key, KZ)


def levels(key, dims, pieces, least, top_value):
    def one(position, parts):
        steps = jax.random.uniform(jax.random.fold_in(jax.random.fold_in(key, 6), position), (parts,), jnp.float32, least / len(pieces), top_value / len(pieces))
        return jnp.repeat(jnp.exp(steps), dims[position] // parts).reshape((-1,) + (1,) * (len(dims) - position - 1))

    factor_of = one(*pieces[0])
    for cut in pieces[1:]:
        factor_of = factor_of * one(*cut)
    return factor_of


def scatter_about(key, extent, spread, limit, pieces=(), kind=jnp.bfloat16):
    values = spread * jax.random.normal(key, extent, jnp.float32)
    if pieces:
        values = values * levels(key, extent, pieces, -0.22, 0.18)
    return jnp.clip(values, -limit, limit).astype(kind)


def setup_inputs(seed: int = 0) -> dict:
    arg_keys = jax.random.split(jax.random.key(seed), 5)
    return {
        "hardness_blocks": scatter_about(arg_keys[0], (NB, KJ, B, B), (B * B) ** -0.5, 0.046875, ((0, 16), (2, 2)), jnp.float32),
        "inverse_blocks": scatter_about(arg_keys[1], (NB, KZ, B, B), 1.0, 6.0, ((0, 16), (2, 2)), jnp.float32),
        "hardness_pattern": draw_hardness_pattern(jax.random.fold_in(arg_keys[4], 71), 0),
        "inverse_pattern": draw_inverse_pattern(jax.random.fold_in(arg_keys[4], 71), 0),
    }


def locate(left_pattern, target_pattern, right_pattern):
    listed = jnp.take(right_pattern, left_pattern, axis=0)
    equal = listed[:, :, None, :] == target_pattern[:, None, :, None]
    width = right_pattern.shape[1]
    slot = jnp.sum(jnp.where(equal, jnp.arange(width, dtype=jnp.int32), 0), axis=3)
    flat = (left_pattern[:, :, None] * width + slot).astype(jnp.int32)
    return flat, jnp.any(equal, axis=3)


def combine(left, flat, present, right):
    lined = right.reshape(right.shape[0] * right.shape[1], right.shape[2], right.shape[3])
    total = jnp.zeros((left.shape[0], flat.shape[2], left.shape[2], right.shape[3]), left.dtype)
    for slot in range(flat.shape[1]):
        chosen = jnp.take(lined, flat[:, slot].reshape(-1), axis=0)
        chosen = chosen.reshape(flat.shape[0], flat.shape[2], right.shape[2], right.shape[3])
        chosen = chosen * present[:, slot, :, None, None].astype(left.dtype)
        total = total + jnp.einsum('irp,ikpd->ikrd', left[:, slot], chosen, precision=lax.Precision.HIGHEST)
    return total


def reference(hardness_blocks, inverse_blocks, hardness_pattern, inverse_pattern):
    flat_one, present_one = locate(hardness_pattern, inverse_pattern, inverse_pattern)
    product = combine(hardness_blocks, flat_one, present_one, inverse_blocks)
    flat_two, present_two = locate(inverse_pattern, inverse_pattern, inverse_pattern)
    return 2.0 * inverse_blocks - combine(inverse_blocks, flat_two, present_two, product)
```

```python
import functools

import jax
import jax.numpy as jnp
from jax import lax
from jax.experimental import pallas as pl
from jax.experimental.pallas import tpu as pltpu
from jax.sharding import PartitionSpec as P

REACH = 5
CHUNKS = 1
VMEM_BYTES = 32 * 1024 * 1024


def with_halo(cells, sides, width):
    for axis, dim in sides:
        count = lax.axis_size(axis)
        ends = count - 1
        head = lax.slice_in_dim(cells, 0, width, axis=dim)
        tail = lax.slice_in_dim(cells, cells.shape[dim] - width, cells.shape[dim], axis=dim)
        cells = jnp.concatenate(
            [
                lax.ppermute(tail, axis, [(i, (i + 1) % count) for i in range(ends)]),
                cells,
                lax.ppermute(head, axis, [((i + 1) % count, i) for i in range(ends)]),
            ],
            axis=dim,
        )
    return cells


def match_slots(left_pattern, target_pattern, right_pattern, base):
    local = left_pattern - base
    listed = jnp.take(right_pattern, local, axis=0)
    equal = listed[:, :, None, :] == target_pattern[:, None, :, None]
    width = right_pattern.shape[1]
    slot = jnp.sum(jnp.where(equal, jnp.arange(width, dtype=jnp.int32), 0), axis=3)
    return local[:, :, None], slot, jnp.any(equal, axis=3)


def locate_blocks(left_pattern, target_pattern, right_pattern, base):
    local, slot, found = match_slots(left_pattern, target_pattern, right_pattern, base)
    width = right_pattern.shape[1]
    return jnp.where(found, local * width + slot, right_pattern.shape[0] * width)


def make_fold(left, flat, total, piece):
    count = piece.shape[2]
    lined = piece.reshape(piece.shape[0] * piece.shape[1], count, piece.shape[3])
    lined = jnp.concatenate([lined, jnp.zeros((1, count, piece.shape[3]), lined.dtype)], axis=0)
    for slot in range(flat.shape[1]):
        chosen = jnp.take(lined, flat[:, slot].reshape(-1), axis=0)
        chosen = chosen.reshape(flat.shape[0], flat.shape[2], count, piece.shape[3])
        total = total + jnp.einsum(
            "irp,ikpd->ikrd", left[:, slot], chosen, precision=lax.Precision.HIGHEST
        )
    return total


def patterns_beside(inverse_pattern, count_rows):
    first_row = lax.axis_index("rows") * count_rows
    padded = jnp.pad(inverse_pattern, ((REACH, REACH), (0, 0)), constant_values=-1)
    beside_all = lax.dynamic_slice_in_dim(padded, first_row, count_rows + 2 * REACH, 0)
    own_pattern = lax.dynamic_slice_in_dim(inverse_pattern, first_row, count_rows, 0)
    return first_row - REACH, beside_all, own_pattern


def general_shards(hardness_blocks, inverse_blocks, hardness_pattern, inverse_pattern):
    count_rows = inverse_blocks.shape[0]
    base, beside_all, own_pattern = patterns_beside(inverse_pattern, count_rows)
    flat_one = locate_blocks(hardness_pattern, own_pattern, beside_all, base)
    flat_two = locate_blocks(own_pattern, own_pattern, beside_all, base)
    empty = jnp.zeros(
        (count_rows, own_pattern.shape[1], inverse_blocks.shape[2], inverse_blocks.shape[3]),
        jnp.float32,
    )
    extended = with_halo(inverse_blocks, (("rows", 0),), REACH)
    product = make_fold(
        hardness_blocks, flat_one, empty, lax.all_gather(extended, "inner", axis=2, tiled=True)
    )
    product_ext = with_halo(product, (("rows", 0),), REACH)
    carried = make_fold(
        inverse_blocks, flat_two, empty, lax.all_gather(product_ext, "inner", axis=2, tiled=True)
    )
    return 2.0 * inverse_blocks - carried


def call(body, outs, name, scratch=(), specs=None, flops=0, nbytes=0):
    params = dict(
        out_shape=outs,
        scratch_shapes=list(scratch),
        compiler_params=pltpu.CompilerParams(vmem_limit_bytes=VMEM_BYTES),
        name=name,
        cost_estimate=pl.CostEstimate(flops=flops, bytes_accessed=nbytes, transcendentals=0),
    )
    if specs is not None:
        params.update(grid=(1,), in_specs=specs)
    return pl.pallas_call(body, **params)


def is_low(shape):
    return lax.broadcasted_iota(jnp.int32, shape, len(shape) - 1) < shape[-1] // 2


def swapped(x):
    return pltpu.roll(x, x.shape[-1] // 2, x.ndim - 1)


def unzip_lanes(a, b):
    low = is_low(a.shape)
    return jnp.where(low, a, swapped(b)), jnp.where(low, swapped(a), b)


def halves(x):
    high = x.astype(jnp.bfloat16)
    return high, (x - high.astype(jnp.float32)).astype(jnp.bfloat16)


def split_columns(z_ref, own_ref, send_ref):
    second = lax.axis_index("inner") == 1
    rows, pairs, half, lanes = own_ref.shape
    for i in range(rows):
        for j in range(pairs):
            turned = z_ref[i, 2 * j : 2 * j + 2].reshape(2 * half, lanes).T
            top, bottom = turned[:half], turned[half:]
            own_ref[i, j] = jnp.where(second, bottom, top)
            send_ref[i, j] = jnp.where(second, top, bottom)


def gather_dot(index_ref, i, right_slots, out_slots, high_ref, low_ref, lhs_high, lhs_low, right, dims):
    depth = high_ref.shape[1]
    for s in range(right_slots):
        for k in range(out_slots):
            at = index_ref[(i * right_slots + s) * out_slots + k]
            place = (pl.ds(k * depth, depth), pl.ds(s * 128, 128))
            lhs_high[place] = high_ref[at]
            lhs_low[place] = low_ref[at]
    dot = functools.partial(
        lax.dot_general, dimension_numbers=(dims, ((), ())), preferred_element_type=jnp.float32
    )
    right_high, right_low = right
    return (
        dot(lhs_high[...], right_low)
        + dot(lhs_low[...], right_high)
        + dot(lhs_high[...], right_high)
    )


def first_product(index_ref, z_own, z_oth, on_own, on_oth, off_own, off_oth, j_own, j_oth, p_ref,
                  z_high, z_low, j_high, j_low, lhs_high, lhs_low):
    second = lax.axis_index("inner") == 1
    rows, pairs, depth, lanes = z_own.shape
    for g, (own, oth) in enumerate(((z_own, z_oth), (on_own, on_oth), (off_own, off_oth))):
        for i in range(rows):
            for j in range(pairs):
                even, odd = unzip_lanes(own[i, j], oth[i, j])
                at = ((g * rows + i) * pairs + j) * 2
                z_high[at], z_low[at] = halves(even)
                z_high[at + 1], z_low[at + 1] = halves(odd)
    z_high[z_high.shape[0] - 1] = jnp.zeros(z_high.shape[1:], jnp.bfloat16)
    z_low[z_low.shape[0] - 1] = jnp.zeros(z_low.shape[1:], jnp.bfloat16)
    slots, half = j_own.shape[1:3]
    for i in range(rows):
        for s in range(slots):
            for part, source in ((0, j_own), (1, j_oth)):
                x = source[i, s]
                place = (i, pl.ds(part * half, half), pl.ds(s * 128, 128))
                j_high[place], j_low[place] = halves(jnp.where(second, swapped(x), x))

    @pl.loop(0, rows)
    def _(i):
        total = gather_dot(index_ref, i, slots, 2 * pairs, z_high, z_low, lhs_high, lhs_low,
                           (j_high[i], j_low[i]), ((1,), (1,)))
        p_ref[i] = total.reshape(p_ref.shape[1:])


def left_blocks(z_own, z_send, z_oth, z_rest, high_ref, low_ref):
    rows, pairs, half, lanes = z_own.shape
    for i in range(rows):
        for j in range(pairs):
            for part, (own, oth) in enumerate(((z_own, z_oth), (z_send, z_rest))):
                for slot, x in enumerate(unzip_lanes(own[i, j], oth[i, j])):
                    place = (i, pl.ds((2 * j + slot) * lanes + part * half, half))
                    high_ref[place], low_ref[place] = halves(x)


def second_product(index_ref, p_own, p_on, p_off, left_high, left_low, own_ref, send_ref,
                   p_high, p_low, lhs_high, lhs_low):
    rows, slots, depth, lanes = p_own.shape
    for g, source in enumerate((p_own, p_on, p_off)):
        for i in range(rows):
            for k in range(slots):
                at = (g * rows + i) * slots + k
                p_high[at], p_low[at] = halves(source[i, k])
    p_high[p_high.shape[0] - 1] = jnp.zeros(p_high.shape[1:], jnp.bfloat16)
    p_low[p_low.shape[0] - 1] = jnp.zeros(p_low.shape[1:], jnp.bfloat16)

    @pl.loop(0, rows)
    def _(i):
        total = gather_dot(index_ref, i, slots, slots, p_high, p_low, lhs_high, lhs_low,
                           (left_high[i], left_low[i]), ((1,), (0,)))
        total = total.reshape(slots, depth, lanes)
        for j in range(slots // 2):
            own_ref[i, j], send_ref[i, j] = unzip_lanes(total[2 * j], total[2 * j + 1])


def finish(chunks, z_ref, *refs):
    second = lax.axis_index("inner") == 1
    own, oth, out_ref = refs[:chunks], refs[chunks : 2 * chunks], refs[-1]
    rows, slots, half, lanes = z_ref.shape
    for i in range(rows):
        for j in range(slots // 2):
            stack = jnp.concatenate([ref[i, j] for ref in own + oth], axis=0)
            turned = stack.T
            turned = jnp.where(second, swapped(turned), turned)
            out_ref[i, 2 * j : 2 * j + 2] = (
                2.0 * z_ref[i, 2 * j : 2 * j + 2] - turned.reshape(2, half, lanes)
            )


def half_shards(hardness_blocks, inverse_blocks, hardness_pattern, inverse_pattern):
    rows, slots, half, lanes = inverse_blocks.shape
    left_slots = hardness_blocks.shape[1]
    pairs = slots // 2
    count = lax.axis_size("rows")
    f32 = functools.partial(jax.ShapeDtypeStruct, dtype=jnp.float32)
    bf16 = functools.partial(jax.ShapeDtypeStruct, dtype=jnp.bfloat16)
    pack = f32((rows, pairs, half, lanes))
    smem = pl.BlockSpec(memory_space=pltpu.SMEM)
    vmem = pl.BlockSpec(memory_space=pltpu.VMEM)

    def across(x):
        return lax.ppermute(x, "inner", [(0, 1), (1, 0)])

    def on_swap(x):
        return lax.ppermute(x, "rows", [(i, i ^ 1) for i in range(count)])

    def off_swap(x):
        inside = [(i, i + 1) for i in range(1, count - 1, 2)]
        return lax.ppermute(x, "rows", inside + [(b, a) for a, b in inside])

    z_own, z_send = call(split_columns, (pack, pack), "split_columns", nbytes=8 << 18)(inverse_blocks)
    z_oth = across(z_send)
    off_own = off_swap(z_own)
    on_own = on_swap(z_own)
    j_oth = across(hardness_blocks)
    off_oth = off_swap(z_oth)
    on_oth = on_swap(z_oth)
    z_rest = across(z_own)

    base, beside_all, own_pattern = patterns_beside(inverse_pattern, rows)
    odd = lax.axis_index("rows") % 2

    def flat_index(left_pattern):
        local, slot, found = match_slots(left_pattern, own_pattern, beside_all, base)
        offset = local - REACH
        segment = jnp.where(offset < 0, 2 - odd, jnp.where(offset < rows, 0, 1 + odd))
        flat = (segment * rows + jnp.where(offset < 0, offset + rows, offset % rows)) * slots + slot
        return jnp.where(found, flat, 3 * rows * slots).astype(jnp.int32).reshape(-1)

    flat_one = flat_index(hardness_pattern)
    flat_two = flat_index(own_pattern)

    left = call(
        left_blocks, (bf16((rows, slots * lanes, lanes)),) * 2, "left_blocks", nbytes=16 << 18
    )(z_own, z_send, z_oth, z_rest)

    depth = half // CHUNKS
    blocks = 3 * rows * slots + 1

    def first(c):
        part = pl.BlockSpec((rows, pairs, depth, lanes), lambda g: (0, 0, c, 0))
        return call(
            first_product,
            f32((rows, slots, depth, lanes)),
            "first_product",
            scratch=[
                pltpu.VMEM((blocks, depth, lanes), jnp.bfloat16),
                pltpu.VMEM((blocks, depth, lanes), jnp.bfloat16),
                pltpu.VMEM((rows, lanes, left_slots * lanes), jnp.bfloat16),
                pltpu.VMEM((rows, lanes, left_slots * lanes), jnp.bfloat16),
                pltpu.VMEM((slots * depth, left_slots * lanes), jnp.bfloat16),
                pltpu.VMEM((slots * depth, left_slots * lanes), jnp.bfloat16),
            ],
            specs=[smem] + [part] * 6 + [vmem] * 2,
            flops=6 * rows * left_slots * slots * depth * lanes * lanes,
            nbytes=16 << 18,
        )(flat_one, z_own, z_oth, on_own, on_oth, off_own, off_oth, hardness_blocks, j_oth)

    def second(p, p_on, p_off):
        return call(
            second_product,
            (f32((rows, pairs, depth, lanes)),) * 2,
            "second_product",
            scratch=[
                pltpu.VMEM((blocks, depth, lanes), jnp.bfloat16),
                pltpu.VMEM((blocks, depth, lanes), jnp.bfloat16),
                pltpu.VMEM((slots * depth, slots * lanes), jnp.bfloat16),
                pltpu.VMEM((slots * depth, slots * lanes), jnp.bfloat16),
            ],
            specs=[smem] + [vmem] * 5,
            flops=6 * rows * slots * slots * depth * lanes * lanes,
            nbytes=16 << 18,
        )(flat_two, p, p_on, p_off, *left)

    products = []
    for c in range(CHUNKS):
        p = first(c)
        products.append((p, on_swap(p), off_swap(p)))
    own, oth = [], []
    for p, p_on, p_off in products:
        mine, send = second(p, p_on, p_off)
        own.append(mine)
        oth.append(across(send))
    return call(
        functools.partial(finish, CHUNKS), f32(inverse_blocks.shape), "finish", nbytes=12 << 18
    )(inverse_blocks, *own, *oth)


def solution(mesh):
    in_specs = (
        P("rows", None, "inner", None),
        P("rows", None, "inner", None),
        P("rows", None),
        P(),
    )
    out_specs = P("rows", None, "inner", None)
    halved = mesh.shape["inner"] == 2 and mesh.shape["rows"] % 2 == 0
    shards = half_shards if halved else general_shards
    return jax.shard_map(shards, mesh=mesh, in_specs=in_specs, out_specs=out_specs, check_vma=False)
```

```python
import functools

import jax
import jax.numpy as jnp
from jax import lax
from jax.experimental import pallas as pl
from jax.experimental.pallas import tpu as pltpu
from jax.sharding import PartitionSpec as P

REACH = 5
CHUNKS = 2
VMEM_BYTES = 32 * 1024 * 1024


def with_halo(cells, sides, width):
    for axis, dim in sides:
        count = lax.axis_size(axis)
        ends = count - 1
        head = lax.slice_in_dim(cells, 0, width, axis=dim)
        tail = lax.slice_in_dim(cells, cells.shape[dim] - width, cells.shape[dim], axis=dim)
        cells = jnp.concatenate(
            [
                lax.ppermute(tail, axis, [(i, (i + 1) % count) for i in range(ends)]),
                cells,
                lax.ppermute(head, axis, [((i + 1) % count, i) for i in range(ends)]),
            ],
            axis=dim,
        )
    return cells


def match_slots(left_pattern, target_pattern, right_pattern, base):
    local = left_pattern - base
    listed = jnp.take(right_pattern, local, axis=0)
    equal = listed[:, :, None, :] == target_pattern[:, None, :, None]
    width = right_pattern.shape[1]
    slot = jnp.sum(jnp.where(equal, jnp.arange(width, dtype=jnp.int32), 0), axis=3)
    return local[:, :, None], slot, jnp.any(equal, axis=3)


def locate_blocks(left_pattern, target_pattern, right_pattern, base):
    local, slot, found = match_slots(left_pattern, target_pattern, right_pattern, base)
    width = right_pattern.shape[1]
    return jnp.where(found, local * width + slot, right_pattern.shape[0] * width)


def make_fold(left, flat, total, piece):
    count = piece.shape[2]
    lined = piece.reshape(piece.shape[0] * piece.shape[1], count, piece.shape[3])
    lined = jnp.concatenate([lined, jnp.zeros((1, count, piece.shape[3]), lined.dtype)], axis=0)
    for slot in range(flat.shape[1]):
        chosen = jnp.take(lined, flat[:, slot].reshape(-1), axis=0)
        chosen = chosen.reshape(flat.shape[0], flat.shape[2], count, piece.shape[3])
        total = total + jnp.einsum(
            "irp,ikpd->ikrd", left[:, slot], chosen, precision=lax.Precision.HIGHEST
        )
    return total


def patterns_beside(inverse_pattern, count_rows):
    first_row = lax.axis_index("rows") * count_rows
    padded = jnp.pad(inverse_pattern, ((REACH, REACH), (0, 0)), constant_values=-1)
    beside_all = lax.dynamic_slice_in_dim(padded, first_row, count_rows + 2 * REACH, 0)
    own_pattern = lax.dynamic_slice_in_dim(inverse_pattern, first_row, count_rows, 0)
    return first_row - REACH, beside_all, own_pattern


def general_shards(hardness_blocks, inverse_blocks, hardness_pattern, inverse_pattern):
    count_rows = inverse_blocks.shape[0]
    base, beside_all, own_pattern = patterns_beside(inverse_pattern, count_rows)
    flat_one = locate_blocks(hardness_pattern, own_pattern, beside_all, base)
    flat_two = locate_blocks(own_pattern, own_pattern, beside_all, base)
    empty = jnp.zeros(
        (count_rows, own_pattern.shape[1], inverse_blocks.shape[2], inverse_blocks.shape[3]),
        jnp.float32,
    )
    extended = with_halo(inverse_blocks, (("rows", 0),), REACH)
    product = make_fold(
        hardness_blocks, flat_one, empty, lax.all_gather(extended, "inner", axis=2, tiled=True)
    )
    product_ext = with_halo(product, (("rows", 0),), REACH)
    carried = make_fold(
        inverse_blocks, flat_two, empty, lax.all_gather(product_ext, "inner", axis=2, tiled=True)
    )
    return 2.0 * inverse_blocks - carried


def call(body, outs, name, scratch=(), specs=None, flops=0, nbytes=0):
    params = dict(
        out_shape=outs,
        scratch_shapes=list(scratch),
        compiler_params=pltpu.CompilerParams(vmem_limit_bytes=VMEM_BYTES),
        name=name,
        cost_estimate=pl.CostEstimate(flops=flops, bytes_accessed=nbytes, transcendentals=0),
    )
    if specs is not None:
        params.update(grid=(1,), in_specs=specs)
    return pl.pallas_call(body, **params)


def is_low(shape):
    return lax.broadcasted_iota(jnp.int32, shape, len(shape) - 1) < shape[-1] // 2


def swapped(x):
    return pltpu.roll(x, x.shape[-1] // 2, x.ndim - 1)


def unzip_lanes(a, b):
    low = is_low(a.shape)
    return jnp.where(low, a, swapped(b)), jnp.where(low, swapped(a), b)


def halves(x):
    high = x.astype(jnp.bfloat16)
    return high, (x - high.astype(jnp.float32)).astype(jnp.bfloat16)


def split_columns(z_ref, own_ref, send_ref):
    second = lax.axis_index("inner") == 1
    rows, pairs, half, lanes = own_ref.shape
    for i in range(rows):
        for j in range(pairs):
            turned = z_ref[i, 2 * j : 2 * j + 2].reshape(2 * half, lanes).T
            top, bottom = turned[:half], turned[half:]
            own_ref[i, j] = jnp.where(second, bottom, top)
            send_ref[i, j] = jnp.where(second, top, bottom)


def gather_dot(index_ref, i, right_slots, out_slots, high_ref, low_ref, lhs_high, lhs_low, right, dims):
    depth = high_ref.shape[1]
    for s in range(right_slots):
        for k in range(out_slots):
            at = index_ref[(i * right_slots + s) * out_slots + k]
            place = (pl.ds(k * depth, depth), pl.ds(s * 128, 128))
            lhs_high[place] = high_ref[at]
            lhs_low[place] = low_ref[at]
    dot = functools.partial(
        lax.dot_general, dimension_numbers=(dims, ((), ())), preferred_element_type=jnp.float32
    )
    right_high, right_low = right
    return (
        dot(lhs_high[...], right_low)
        + dot(lhs_low[...], right_high)
        + dot(lhs_high[...], right_high)
    )


def first_product(index_ref, z_own, z_oth, on_own, on_oth, off_own, off_oth, j_own, j_oth, p_ref,
                  z_high, z_low, j_high, j_low, lhs_high, lhs_low):
    second = lax.axis_index("inner") == 1
    rows, pairs, depth, lanes = z_own.shape
    for g, (own, oth) in enumerate(((z_own, z_oth), (on_own, on_oth), (off_own, off_oth))):
        for i in range(rows):
            for j in range(pairs):
                even, odd = unzip_lanes(own[i, j], oth[i, j])
                at = ((g * rows + i) * pairs + j) * 2
                z_high[at], z_low[at] = halves(even)
                z_high[at + 1], z_low[at + 1] = halves(odd)
    z_high[z_high.shape[0] - 1] = jnp.zeros(z_high.shape[1:], jnp.bfloat16)
    z_low[z_low.shape[0] - 1] = jnp.zeros(z_low.shape[1:], jnp.bfloat16)
    slots, half = j_own.shape[1:3]
    for i in range(rows):
        for s in range(slots):
            for part, source in ((0, j_own), (1, j_oth)):
                x = source[i, s]
                place = (i, pl.ds(part * half, half), pl.ds(s * 128, 128))
                j_high[place], j_low[place] = halves(jnp.where(second, swapped(x), x))

    @pl.loop(0, rows)
    def _(i):
        total = gather_dot(index_ref, i, slots, 2 * pairs, z_high, z_low, lhs_high, lhs_low,
                           (j_high[i], j_low[i]), ((1,), (1,)))
        p_ref[i] = total.reshape(p_ref.shape[1:])


def left_blocks(z_own, z_send, z_oth, z_rest, high_ref, low_ref):
    rows, pairs, half, lanes = z_own.shape
    for i in range(rows):
        for j in range(pairs):
            for part, (own, oth) in enumerate(((z_own, z_oth), (z_send, z_rest))):
                for slot, x in enumerate(unzip_lanes(own[i, j], oth[i, j])):
                    place = (i, pl.ds((2 * j + slot) * lanes + part * half, half))
                    high_ref[place], low_ref[place] = halves(x)


def second_product(index_ref, p_own, p_on, p_off, left_high, left_low, own_ref, send_ref,
                   p_high, p_low, lhs_high, lhs_low):
    rows, slots, depth, lanes = p_own.shape
    for g, source in enumerate((p_own, p_on, p_off)):
        for i in range(rows):
            for k in range(slots):
                at = (g * rows + i) * slots + k
                p_high[at], p_low[at] = halves(source[i, k])
    p_high[p_high.shape[0] - 1] = jnp.zeros(p_high.shape[1:], jnp.bfloat16)
    p_low[p_low.shape[0] - 1] = jnp.zeros(p_low.shape[1:], jnp.bfloat16)

    @pl.loop(0, rows)
    def _(i):
        total = gather_dot(index_ref, i, slots, slots, p_high, p_low, lhs_high, lhs_low,
                           (left_high[i], left_low[i]), ((1,), (0,)))
        total = total.reshape(slots, depth, lanes)
        for j in range(slots // 2):
            own_ref[i, j], send_ref[i, j] = unzip_lanes(total[2 * j], total[2 * j + 1])


def finish(chunks, z_ref, *refs):
    second = lax.axis_index("inner") == 1
    own, oth, out_ref = refs[:chunks], refs[chunks : 2 * chunks], refs[-1]
    rows, slots, half, lanes = z_ref.shape
    for i in range(rows):
        for j in range(slots // 2):
            stack = jnp.concatenate([ref[i, j] for ref in own + oth], axis=0)
            turned = stack.T
            turned = jnp.where(second, swapped(turned), turned)
            out_ref[i, 2 * j : 2 * j + 2] = (
                2.0 * z_ref[i, 2 * j : 2 * j + 2] - turned.reshape(2, half, lanes)
            )


def half_shards(hardness_blocks, inverse_blocks, hardness_pattern, inverse_pattern):
    rows, slots, half, lanes = inverse_blocks.shape
    left_slots = hardness_blocks.shape[1]
    pairs = slots // 2
    count = lax.axis_size("rows")
    f32 = functools.partial(jax.ShapeDtypeStruct, dtype=jnp.float32)
    bf16 = functools.partial(jax.ShapeDtypeStruct, dtype=jnp.bfloat16)
    pack = f32((rows, pairs, half, lanes))
    smem = pl.BlockSpec(memory_space=pltpu.SMEM)
    vmem = pl.BlockSpec(memory_space=pltpu.VMEM)

    def across(x):
        return lax.ppermute(x, "inner", [(0, 1), (1, 0)])

    def on_swap(x):
        return lax.ppermute(x, "rows", [(i, i ^ 1) for i in range(count)])

    def off_swap(x):
        inside = [(i, i + 1) for i in range(1, count - 1, 2)]
        return lax.ppermute(x, "rows", inside + [(b, a) for a, b in inside])

    z_own, z_send = call(split_columns, (pack, pack), "split_columns", nbytes=8 << 18)(inverse_blocks)
    z_oth = across(z_send)
    off_own = off_swap(z_own)
    on_own = on_swap(z_own)
    later, on_own = lax.optimization_barrier((hardness_blocks, on_own))
    j_oth = across(later)
    off_oth = off_swap(z_oth)
    on_oth = on_swap(z_oth)
    later, on_oth = lax.optimization_barrier((z_own, on_oth))
    z_rest = across(later)

    base, beside_all, own_pattern = patterns_beside(inverse_pattern, rows)
    odd = lax.axis_index("rows") % 2

    def flat_index(left_pattern):
        local, slot, found = match_slots(left_pattern, own_pattern, beside_all, base)
        offset = local - REACH
        segment = jnp.where(offset < 0, 2 - odd, jnp.where(offset < rows, 0, 1 + odd))
        flat = (segment * rows + jnp.where(offset < 0, offset + rows, offset % rows)) * slots + slot
        return jnp.where(found, flat, 3 * rows * slots).astype(jnp.int32).reshape(-1)

    flat_one = flat_index(hardness_pattern)
    flat_two = flat_index(own_pattern)

    left = call(
        left_blocks, (bf16((rows, slots * lanes, lanes)),) * 2, "left_blocks", nbytes=16 << 18
    )(z_own, z_send, z_oth, z_rest)

    depth = half // CHUNKS
    blocks = 3 * rows * slots + 1

    def first(c):
        part = pl.BlockSpec((rows, pairs, depth, lanes), lambda g: (0, 0, c, 0))
        return call(
            first_product,
            f32((rows, slots, depth, lanes)),
            "first_product",
            scratch=[
                pltpu.VMEM((blocks, depth, lanes), jnp.bfloat16),
                pltpu.VMEM((blocks, depth, lanes), jnp.bfloat16),
                pltpu.VMEM((rows, lanes, left_slots * lanes), jnp.bfloat16),
                pltpu.VMEM((rows, lanes, left_slots * lanes), jnp.bfloat16),
                pltpu.VMEM((slots * depth, left_slots * lanes), jnp.bfloat16),
                pltpu.VMEM((slots * depth, left_slots * lanes), jnp.bfloat16),
            ],
            specs=[smem] + [part] * 6 + [vmem] * 2,
            flops=6 * rows * left_slots * slots * depth * lanes * lanes,
            nbytes=16 << 18,
        )(flat_one, z_own, z_oth, on_own, on_oth, off_own, off_oth, hardness_blocks, j_oth)

    def second(p, p_on, p_off):
        return call(
            second_product,
            (f32((rows, pairs, depth, lanes)),) * 2,
            "second_product",
            scratch=[
                pltpu.VMEM((blocks, depth, lanes), jnp.bfloat16),
                pltpu.VMEM((blocks, depth, lanes), jnp.bfloat16),
                pltpu.VMEM((slots * depth, slots * lanes), jnp.bfloat16),
                pltpu.VMEM((slots * depth, slots * lanes), jnp.bfloat16),
            ],
            specs=[smem] + [vmem] * 5,
            flops=6 * rows * slots * slots * depth * lanes * lanes,
            nbytes=16 << 18,
        )(flat_two, p, p_on, p_off, *left)

    products = []
    for c in range(CHUNKS):
        p = first(c)
        products.append((p, on_swap(p), off_swap(p)))
    own, oth = [], []
    for p, p_on, p_off in products:
        mine, send = second(p, p_on, p_off)
        own.append(mine)
        oth.append(across(send))
    return call(
        functools.partial(finish, CHUNKS), f32(inverse_blocks.shape), "finish", nbytes=12 << 18
    )(inverse_blocks, *own, *oth)


def solution(mesh):
    in_specs = (
        P("rows", None, "inner", None),
        P("rows", None, "inner", None),
        P("rows", None),
        P(),
    )
    out_specs = P("rows", None, "inner", None)
    halved = mesh.shape["inner"] == 2 and mesh.shape["rows"] % 2 == 0
    shards = half_shards if halved else general_shards
    return jax.shard_map(shards, mesh=mesh, in_specs=in_specs, out_specs=out_specs, check_vma=False)
```

```python
import functools

import jax
import jax.numpy as jnp
from jax import lax
from jax.experimental import pallas as pl
from jax.experimental.pallas import tpu as pltpu
from jax.sharding import PartitionSpec as P

REACH = 5
CHUNKS = (32, 32)
VMEM_BYTES = 14 * 1024 * 1024


def with_halo(cells, sides, width):
    for axis, dim in sides:
        count = lax.axis_size(axis)
        ends = count - 1
        head = lax.slice_in_dim(cells, 0, width, axis=dim)
        tail = lax.slice_in_dim(cells, cells.shape[dim] - width, cells.shape[dim], axis=dim)
        cells = jnp.concatenate(
            [
                lax.ppermute(tail, axis, [(i, (i + 1) % count) for i in range(ends)]),
                cells,
                lax.ppermute(head, axis, [((i + 1) % count, i) for i in range(ends)]),
            ],
            axis=dim,
        )
    return cells


def match_slots(left_pattern, target_pattern, right_pattern, base):
    local = left_pattern - base
    listed = jnp.take(right_pattern, local, axis=0)
    equal = listed[:, :, None, :] == target_pattern[:, None, :, None]
    width = right_pattern.shape[1]
    slot = jnp.sum(jnp.where(equal, jnp.arange(width, dtype=jnp.int32), 0), axis=3)
    return local[:, :, None], slot, jnp.any(equal, axis=3)


def locate_blocks(left_pattern, target_pattern, right_pattern, base):
    local, slot, found = match_slots(left_pattern, target_pattern, right_pattern, base)
    width = right_pattern.shape[1]
    return jnp.where(found, local * width + slot, right_pattern.shape[0] * width)


def make_fold(left, flat, total, piece):
    count = piece.shape[2]
    lined = piece.reshape(piece.shape[0] * piece.shape[1], count, piece.shape[3])
    lined = jnp.concatenate([lined, jnp.zeros((1, count, piece.shape[3]), lined.dtype)], axis=0)
    for slot in range(flat.shape[1]):
        chosen = jnp.take(lined, flat[:, slot].reshape(-1), axis=0)
        chosen = chosen.reshape(flat.shape[0], flat.shape[2], count, piece.shape[3])
        total = total + jnp.einsum(
            "irp,ikpd->ikrd", left[:, slot], chosen, precision=lax.Precision.HIGHEST
        )
    return total


def patterns_beside(inverse_pattern, count_rows):
    first_row = lax.axis_index("rows") * count_rows
    padded = jnp.pad(inverse_pattern, ((REACH, REACH), (0, 0)), constant_values=-1)
    beside_all = lax.dynamic_slice_in_dim(padded, first_row, count_rows + 2 * REACH, 0)
    own_pattern = lax.dynamic_slice_in_dim(inverse_pattern, first_row, count_rows, 0)
    return first_row - REACH, beside_all, own_pattern


def general_shards(hardness_blocks, inverse_blocks, hardness_pattern, inverse_pattern):
    count_rows = inverse_blocks.shape[0]
    base, beside_all, own_pattern = patterns_beside(inverse_pattern, count_rows)
    flat_one = locate_blocks(hardness_pattern, own_pattern, beside_all, base)
    flat_two = locate_blocks(own_pattern, own_pattern, beside_all, base)
    empty = jnp.zeros(
        (count_rows, own_pattern.shape[1], inverse_blocks.shape[2], inverse_blocks.shape[3]),
        jnp.float32,
    )
    extended = with_halo(inverse_blocks, (("rows", 0),), REACH)
    product = make_fold(
        hardness_blocks, flat_one, empty, lax.all_gather(extended, "inner", axis=2, tiled=True)
    )
    product_ext = with_halo(product, (("rows", 0),), REACH)
    carried = make_fold(
        inverse_blocks, flat_two, empty, lax.all_gather(product_ext, "inner", axis=2, tiled=True)
    )
    return 2.0 * inverse_blocks - carried


def call(body, outs, name, scratch=(), specs=None, out_specs=None, flops=0, nbytes=0):
    params = dict(
        out_shape=outs,
        scratch_shapes=list(scratch),
        compiler_params=pltpu.CompilerParams(vmem_limit_bytes=VMEM_BYTES),
        name=name,
        cost_estimate=pl.CostEstimate(flops=flops, bytes_accessed=nbytes, transcendentals=0),
    )
    if specs is not None:
        params.update(in_specs=specs)
    if out_specs is not None:
        params.update(out_specs=out_specs)
    return pl.pallas_call(body, **params)


def is_low(shape):
    return lax.broadcasted_iota(jnp.int32, shape, len(shape) - 1) < shape[-1] // 2


def swapped(x):
    return pltpu.roll(x, x.shape[-1] // 2, x.ndim - 1)


def unzip_lanes(a, b):
    low = is_low(a.shape)
    return jnp.where(low, a, swapped(b)), jnp.where(low, swapped(a), b)


def halves(x):
    high = x.astype(jnp.bfloat16)
    return high, (x - high.astype(jnp.float32)).astype(jnp.bfloat16)


def find_blocks(left_ref, pattern_ref, one_ref, two_ref, table):
    rows = left_ref.shape[0]
    slots = pattern_ref.shape[1]
    device = lax.axis_index("rows")
    first = device * rows
    last = pattern_ref.shape[0] - 1
    odd = device % 2
    width = 2 * REACH + 1
    none = 3 * rows * slots

    @pl.loop(0, table.shape[0])
    def _(n):
        table[n] = none

    def segment(n):
        return (2 - odd, 0, 1 + odd)[n]

    for n in range(3):
        base = segment(n) * rows

        @pl.loop(0, rows)
        def _(r):
            local = (n - 1) * rows + r
            row = jnp.clip(first + local, 0, last)
            for k in range(slots):
                shift = pattern_ref[row, k] - row + REACH
                table[(local + rows) * width + shift] = (base + r) * slots + k

    def look_up(i, row, k):
        column = pattern_ref[first + i, k]
        shift = column - row + REACH
        inside = (shift >= 0) & (shift < width)
        found = table[(row - first + rows) * width + jnp.clip(shift, 0, width - 1)]
        return jnp.where(inside, found, none)

    @pl.loop(0, rows)
    def _(i):
        for count, row_of, out_ref in (
            (left_ref.shape[1], lambda s: left_ref[i, s], one_ref),
            (slots, lambda m: pattern_ref[first + i, m], two_ref),
        ):
            for s in range(count):
                row = row_of(s)
                for k in range(slots):
                    out_ref[(i * count + s) * slots + k] = look_up(i, row, k)


def split_columns(send, z_ref, *refs):
    out_ref = refs[-1]
    second = lax.axis_index("inner") == 1
    rows, pairs, half, lanes = out_ref.shape
    for i in range(rows):
        for j in range(pairs):
            turned = z_ref[i, 2 * j : 2 * j + 2].reshape(2 * half, lanes).T
            top, bottom = turned[:half], turned[half:]
            out_ref[i, j] = jnp.where(second, top, bottom) if send else jnp.where(second, bottom, top)


def gather_dot(index_ref, i, right_slots, out_slots, high_ref, low_ref, lhs_high, lhs_low, right, dims):
    depth = high_ref.shape[1]
    for s in range(right_slots):
        for k in range(out_slots):
            at = index_ref[(i * right_slots + s) * out_slots + k]
            place = (pl.ds(k * depth, depth), pl.ds(s * 128, 128))
            lhs_high[place] = high_ref[at]
            lhs_low[place] = low_ref[at]
    dot = functools.partial(
        lax.dot_general, dimension_numbers=(dims, ((), ())), preferred_element_type=jnp.float32
    )
    right_high, right_low = right
    return (
        dot(lhs_high[...], right_low)
        + dot(lhs_low[...], right_high)
        + dot(lhs_high[...], right_high)
    )


def turn_lanes(x):
    return jnp.where(lax.axis_index("inner") == 1, swapped(x), x)


def left_rows(j_ref, high_ref, low_ref):
    for i in range(j_ref.shape[0]):
        for s in range(j_ref.shape[1]):
            place = (i, slice(None), pl.ds(s * 128, 128))
            high_ref[place], low_ref[place] = halves(turn_lanes(j_ref[i, s]))


def merge_near(z_own, z_oth, on_own, on_oth, high_ref, low_ref):
    rows, pairs, half, lanes = z_own.shape
    for g, (own, oth) in enumerate(((z_own, z_oth), (on_own, on_oth))):
        for i in range(rows):
            for j in range(pairs):
                at = ((g * rows + i) * pairs + j) * 2
                even, odd = unzip_lanes(own[i, j], oth[i, j])
                high_ref[at], low_ref[at] = halves(even)
                high_ref[at + 1], low_ref[at + 1] = halves(odd)


def first_product(index_ref, near_high, near_low, off_own, off_oth, j_own_high, j_own_low, j_oth, *refs):
    *p_refs, off_in, z_high, z_low, j_high, j_low, lhs_high, lhs_low, sems = refs
    rows, pairs, half, lanes = off_oth.shape
    slots = j_oth.shape[1]
    near = near_high.shape[0]
    copies = [
        pltpu.make_async_copy(src, dst, sems.at[n])
        for n, (src, dst) in enumerate((
            (off_own, off_in),
            (near_high, z_high.at[pl.ds(0, near)]),
            (near_low, z_low.at[pl.ds(0, near)]),
            (j_own_high, j_high.at[:, pl.ds(0, half)]),
            (j_own_low, j_low.at[:, pl.ds(0, half)]),
        ))
    ]
    for copy in copies:
        copy.start()
    blank = z_high.shape[0] - 1
    z_high[blank] = jnp.zeros(z_high.shape[1:], jnp.bfloat16)
    z_low[blank] = jnp.zeros(z_low.shape[1:], jnp.bfloat16)
    for i in range(rows):
        for s in range(slots):
            place = (i, pl.ds(half, half), pl.ds(s * 128, 128))
            j_high[place], j_low[place] = halves(turn_lanes(j_oth[i, s]))
    copies[0].wait()
    for i in range(rows):
        for j in range(pairs):
            even, odd = unzip_lanes(off_in[i, j], off_oth[i, j])
            at = near + (i * pairs + j) * 2
            z_high[at], z_low[at] = halves(even)
            z_high[at + 1], z_low[at + 1] = halves(odd)
    for copy in copies[1:]:
        copy.wait()
    for i in range(rows):
        total = gather_dot(index_ref, i, slots, 2 * pairs, z_high, z_low, lhs_high, lhs_low,
                           (j_high[i], j_low[i]), ((1,), (1,)))
        total = total.reshape(2 * pairs, half, lanes)
        start = 0
        for p_ref in p_refs:
            depth = p_ref.shape[2]
            p_ref[i] = total[:, start : start + depth]
            start += depth


def left_blocks(z_own, z_send, z_oth, z_rest, high_ref, low_ref):
    rows, pairs, half, lanes = z_own.shape
    for i in range(rows):
        for j in range(pairs):
            for part, (own, oth) in enumerate(((z_own, z_oth), (z_send, z_rest))):
                for slot, x in enumerate(unzip_lanes(own[i, j], oth[i, j])):
                    place = (i, pl.ds((2 * j + slot) * lanes + part * half, half))
                    high_ref[place], low_ref[place] = halves(x)


def second_product(index_ref, p_own, p_on, p_off, l_high, l_low, own_ref, send_ref,
                   p_high, p_low, lhs_high, lhs_low):
    rows, slots, depth, lanes = p_own.shape
    blank = p_high.shape[0] - 1
    p_high[blank] = jnp.zeros(p_high.shape[1:], jnp.bfloat16)
    p_low[blank] = jnp.zeros(p_low.shape[1:], jnp.bfloat16)
    for g, source in enumerate((p_own, p_on, p_off)):
        for i in range(rows):
            for k in range(slots):
                at = (g * rows + i) * slots + k
                p_high[at], p_low[at] = halves(source[i, k])
    for i in range(rows):
        total = gather_dot(index_ref, i, slots, slots, p_high, p_low, lhs_high, lhs_low,
                           (l_high[i], l_low[i]), ((1,), (0,)))
        total = total.reshape(slots, depth, lanes)
        for j in range(slots // 2):
            own_ref[i, j], send_ref[i, j] = unzip_lanes(total[2 * j], total[2 * j + 1])


def finish(chunks, z_ref, *refs):
    second = lax.axis_index("inner") == 1
    own, oth, (out_ref, staged, sems) = refs[:chunks], refs[chunks : 2 * chunks], refs[2 * chunks :]
    rows, slots, half, lanes = z_ref.shape
    copies = []
    for i in range(rows):
        for j in range(slots // 2):
            stack = jnp.concatenate([ref[i, j] for ref in own + oth], axis=0)
            turned = stack.T
            turned = jnp.where(second, swapped(turned), turned)
            staged[i, 2 * j : 2 * j + 2] = (
                2.0 * z_ref[i, 2 * j : 2 * j + 2] - turned.reshape(2, half, lanes)
            )
        copies.append(pltpu.make_async_copy(staged.at[i], out_ref.at[i], sems.at[i]))
        copies[-1].start()
    for copy in copies:
        copy.wait()


def half_shards(hardness_blocks, inverse_blocks, hardness_pattern, inverse_pattern):
    rows, slots, half, lanes = inverse_blocks.shape
    left_slots = hardness_blocks.shape[1]
    pairs = slots // 2
    count = lax.axis_size("rows")
    f32 = functools.partial(jax.ShapeDtypeStruct, dtype=jnp.float32)
    bf16 = functools.partial(jax.ShapeDtypeStruct, dtype=jnp.bfloat16)
    pack = f32((rows, pairs, half, lanes))
    smem = pl.BlockSpec(memory_space=pltpu.SMEM)
    vmem = pl.BlockSpec(memory_space=pltpu.VMEM)
    hbm = pl.BlockSpec(memory_space=pltpu.HBM)
    anywhere = pl.BlockSpec(memory_space=pl.ANY)

    def across(x):
        return lax.ppermute(x, "inner", [(0, 1), (1, 0)])

    def on_swap(x):
        return lax.ppermute(x, "rows", [(i, i ^ 1) for i in range(count)])

    def off_swap(x):
        inside = [(i, i + 1) for i in range(1, count - 1, 2)]
        return lax.ppermute(x, "rows", inside + [(b, a) for a, b in inside])

    z_send = call(functools.partial(split_columns, True), pack, "split_send", nbytes=6 << 18)(inverse_blocks)
    z_own = call(
        functools.partial(split_columns, False), pack, "split_own", specs=[vmem, anywhere], nbytes=6 << 18
    )(inverse_blocks, z_send)
    z_oth = across(z_send)
    off_own = off_swap(z_own)
    on_own = on_swap(z_own)
    off_oth = off_swap(z_oth)
    on_oth = on_swap(z_oth)
    later, z_oth = lax.optimization_barrier((z_own, z_oth))
    z_rest = across(later)

    inverse_pattern, z_oth = lax.optimization_barrier((inverse_pattern, z_oth))
    flat_one, flat_two = call(
        find_blocks,
        (
            jax.ShapeDtypeStruct((rows * left_slots * slots,), jnp.int32),
            jax.ShapeDtypeStruct((rows * slots * slots,), jnp.int32),
        ),
        "find_blocks",
        scratch=[pltpu.SMEM((3 * rows * (2 * REACH + 1),), jnp.int32)],
        specs=[smem, smem],
        out_specs=[smem, smem],
    )(hardness_pattern, inverse_pattern)
    later, z_own = lax.optimization_barrier((hardness_blocks, z_own))
    j_oth = across(later)

    later, off_own = lax.optimization_barrier((hardness_blocks, off_own))
    j_own = call(
        left_rows, (bf16((rows, half, left_slots * lanes)),) * 2, "left_rows", nbytes=4 << 18
    )(later)

    left = call(
        left_blocks, (bf16((rows, slots * lanes, lanes)),) * 2, "left_blocks", nbytes=16 << 18
    )(z_own, z_send, z_oth, z_rest)

    blocks = 3 * rows * slots + 1
    bf16_buffer = functools.partial(pltpu.VMEM, dtype=jnp.bfloat16)

    near = call(
        merge_near, (bf16((2 * rows * slots, half, lanes)),) * 2, "merge_near", nbytes=16 << 18
    )(z_own, z_oth, on_own, on_oth)
    products = call(
        first_product,
        tuple(f32((rows, slots, depth, lanes)) for depth in CHUNKS),
        "first_product",
        scratch=[pltpu.VMEM((rows, pairs, half, lanes), jnp.float32)]
        + [bf16_buffer((blocks, half, lanes))] * 2
        + [bf16_buffer((rows, lanes, left_slots * lanes))] * 2
        + [bf16_buffer((slots * half, left_slots * lanes))] * 2
        + [pltpu.SemaphoreType.DMA((5,))],
        specs=[smem, hbm, hbm, hbm, vmem, hbm, hbm, vmem],
        flops=6 * rows * left_slots * slots * half * lanes * lanes,
        nbytes=16 << 18,
    )(flat_one, *near, off_own, off_oth, *j_own, j_oth)
    products = [(p, on_swap(p), off_swap(p)) for p in products]

    def second(p, p_on, p_off):
        depth = p.shape[2]
        return call(
            second_product,
            (f32((rows, pairs, depth, lanes)),) * 2,
            "second_product",
            scratch=[bf16_buffer((blocks, depth, lanes))] * 2
            + [bf16_buffer((slots * depth, slots * lanes))] * 2,
            specs=[smem] + [vmem] * 5,
            flops=6 * rows * slots * slots * depth * lanes * lanes,
            nbytes=16 << 18,
        )(flat_two, p, p_on, p_off, *left)

    own, oth = [], []
    for p, p_on, p_off in products:
        mine, send = second(p, p_on, p_off)
        own.append(mine)
        oth.append(across(send))
    return call(
        functools.partial(finish, len(CHUNKS)),
        f32(inverse_blocks.shape),
        "finish",
        scratch=[pltpu.VMEM(inverse_blocks.shape, jnp.float32), pltpu.SemaphoreType.DMA((rows,))],
        specs=[vmem] * (1 + 2 * len(CHUNKS)),
        out_specs=anywhere,
        nbytes=12 << 18,
    )(inverse_blocks, *own, *oth)


def solution(mesh):
    in_specs = (
        P("rows", None, "inner", None),
        P("rows", None, "inner", None),
        P("rows", None),
        P(),
    )
    out_specs = P("rows", None, "inner", None)
    halved = mesh.shape["inner"] == 2 and mesh.shape["rows"] % 2 == 0
    shards = half_shards if halved else general_shards
    return jax.shard_map(shards, mesh=mesh, in_specs=in_specs, out_specs=out_specs, check_vma=False)
```

```python
import functools

import jax
import jax.numpy as jnp
from jax import lax
from jax.experimental import pallas as pl
from jax.experimental.pallas import tpu as pltpu
from jax.sharding import PartitionSpec as P

REACH = 5
CHUNKS = (32, 32)
VMEM_BYTES = 14 * 1024 * 1024


def with_halo(cells, sides, width):
    for axis, dim in sides:
        count = lax.axis_size(axis)
        ends = count - 1
        head = lax.slice_in_dim(cells, 0, width, axis=dim)
        tail = lax.slice_in_dim(cells, cells.shape[dim] - width, cells.shape[dim], axis=dim)
        cells = jnp.concatenate(
            [
                lax.ppermute(tail, axis, [(i, (i + 1) % count) for i in range(ends)]),
                cells,
                lax.ppermute(head, axis, [((i + 1) % count, i) for i in range(ends)]),
            ],
            axis=dim,
        )
    return cells


def match_slots(left_pattern, target_pattern, right_pattern, base):
    local = left_pattern - base
    listed = jnp.take(right_pattern, local, axis=0)
    equal = listed[:, :, None, :] == target_pattern[:, None, :, None]
    width = right_pattern.shape[1]
    slot = jnp.sum(jnp.where(equal, jnp.arange(width, dtype=jnp.int32), 0), axis=3)
    return local[:, :, None], slot, jnp.any(equal, axis=3)


def locate_blocks(left_pattern, target_pattern, right_pattern, base):
    local, slot, found = match_slots(left_pattern, target_pattern, right_pattern, base)
    width = right_pattern.shape[1]
    return jnp.where(found, local * width + slot, right_pattern.shape[0] * width)


def make_fold(left, flat, total, piece):
    count = piece.shape[2]
    lined = piece.reshape(piece.shape[0] * piece.shape[1], count, piece.shape[3])
    lined = jnp.concatenate([lined, jnp.zeros((1, count, piece.shape[3]), lined.dtype)], axis=0)
    for slot in range(flat.shape[1]):
        chosen = jnp.take(lined, flat[:, slot].reshape(-1), axis=0)
        chosen = chosen.reshape(flat.shape[0], flat.shape[2], count, piece.shape[3])
        total = total + jnp.einsum(
            "irp,ikpd->ikrd", left[:, slot], chosen, precision=lax.Precision.HIGHEST
        )
    return total


def patterns_beside(inverse_pattern, count_rows):
    first_row = lax.axis_index("rows") * count_rows
    padded = jnp.pad(inverse_pattern, ((REACH, REACH), (0, 0)), constant_values=-1)
    beside_all = lax.dynamic_slice_in_dim(padded, first_row, count_rows + 2 * REACH, 0)
    own_pattern = lax.dynamic_slice_in_dim(inverse_pattern, first_row, count_rows, 0)
    return first_row - REACH, beside_all, own_pattern


def general_shards(hardness_blocks, inverse_blocks, hardness_pattern, inverse_pattern):
    count_rows = inverse_blocks.shape[0]
    base, beside_all, own_pattern = patterns_beside(inverse_pattern, count_rows)
    flat_one = locate_blocks(hardness_pattern, own_pattern, beside_all, base)
    flat_two = locate_blocks(own_pattern, own_pattern, beside_all, base)
    empty = jnp.zeros(
        (count_rows, own_pattern.shape[1], inverse_blocks.shape[2], inverse_blocks.shape[3]),
        jnp.float32,
    )
    extended = with_halo(inverse_blocks, (("rows", 0),), REACH)
    product = make_fold(
        hardness_blocks, flat_one, empty, lax.all_gather(extended, "inner", axis=2, tiled=True)
    )
    product_ext = with_halo(product, (("rows", 0),), REACH)
    carried = make_fold(
        inverse_blocks, flat_two, empty, lax.all_gather(product_ext, "inner", axis=2, tiled=True)
    )
    return 2.0 * inverse_blocks - carried


def call(body, outs, name, scratch=(), specs=None, out_specs=None, flops=0, nbytes=0):
    params = dict(
        out_shape=outs,
        scratch_shapes=list(scratch),
        compiler_params=pltpu.CompilerParams(vmem_limit_bytes=VMEM_BYTES),
        name=name,
        cost_estimate=pl.CostEstimate(flops=flops, bytes_accessed=nbytes, transcendentals=0),
    )
    if specs is not None:
        params.update(in_specs=specs)
    if out_specs is not None:
        params.update(out_specs=out_specs)
    return pl.pallas_call(body, **params)


def is_low(shape):
    return lax.broadcasted_iota(jnp.int32, shape, len(shape) - 1) < shape[-1] // 2


def swapped(x):
    return pltpu.roll(x, x.shape[-1] // 2, x.ndim - 1)


def unzip_lanes(a, b):
    low = is_low(a.shape)
    return jnp.where(low, a, swapped(b)), jnp.where(low, swapped(a), b)


def halves(x):
    high = x.astype(jnp.bfloat16)
    return high, (x - high.astype(jnp.float32)).astype(jnp.bfloat16)


def find_blocks(left_ref, pattern_ref, one_ref, two_ref, table):
    rows = left_ref.shape[0]
    slots = pattern_ref.shape[1]
    device = lax.axis_index("rows")
    first = device * rows
    last = pattern_ref.shape[0] - 1
    odd = device % 2
    width = 2 * REACH + 1
    none = 3 * rows * slots

    @pl.loop(0, 3 * rows)
    def _(n):
        for shift in range(width):
            table[n * width + shift] = none

    for n, segment in enumerate((2 - odd, 0, 1 + odd)):

        @pl.loop(0, rows)
        def _(r):
            local = n * rows + r
            row = jnp.clip(first + local - rows, 0, last)
            shifts = [pattern_ref[row, k] - row + REACH for k in range(slots)]
            for k, shift in enumerate(shifts):
                table[local * width + shift] = (segment * rows + r) * slots + k

    @pl.loop(0, rows)
    def _(i):
        columns = [pattern_ref[first + i, k] for k in range(slots)]
        for count, lefts, out_ref in (
            (left_ref.shape[1], [left_ref[i, s] for s in range(left_ref.shape[1])], one_ref),
            (slots, columns, two_ref),
        ):
            found = []
            for row in lefts:
                at = (row - first + rows) * width
                for column in columns:
                    shift = column - row + REACH
                    inside = (shift >= 0) & (shift < width)
                    found.append(jnp.where(inside, table[at + jnp.clip(shift, 0, width - 1)], none))
            for n, value in enumerate(found):
                out_ref[i * count * slots + n] = value


def split_columns(send, z_ref, *refs):
    out_refs = refs[0 if send else 1 :]
    second = lax.axis_index("inner") == 1
    rows, slots, half, lanes = z_ref.shape
    for i in range(rows):
        for j in range(slots // 2):
            turned = z_ref[i, 2 * j : 2 * j + 2].reshape(2 * half, lanes).T
            top, bottom = turned[:half], turned[half:]
            part = jnp.where(second, top, bottom) if send else jnp.where(second, bottom, top)
            start = 0
            for out_ref in out_refs:
                depth = out_ref.shape[2]
                out_ref[i, j] = part[start : start + depth]
                start += depth


def gather_dot(index_ref, i, right_slots, out_slots, high_ref, low_ref, lhs_high, lhs_low, right, dims):
    depth = high_ref.shape[1]
    for s in range(right_slots):
        for k in range(out_slots):
            at = index_ref[(i * right_slots + s) * out_slots + k]
            place = (pl.ds(k * depth, depth), pl.ds(s * 128, 128))
            lhs_high[place] = high_ref[at]
            lhs_low[place] = low_ref[at]
    dot = functools.partial(
        lax.dot_general, dimension_numbers=(dims, ((), ())), preferred_element_type=jnp.float32
    )
    right_high, right_low = right
    return (
        dot(lhs_high[...], right_low)
        + dot(lhs_low[...], right_high)
        + dot(lhs_high[...], right_high)
    )


def turn_lanes(x):
    return jnp.where(lax.axis_index("inner") == 1, swapped(x), x)


def left_rows(j_ref, high_ref, low_ref):
    for i in range(j_ref.shape[0]):
        for s in range(j_ref.shape[1]):
            place = (i, slice(None), pl.ds(s * 128, 128))
            high_ref[place], low_ref[place] = halves(turn_lanes(j_ref[i, s]))


def merge_near(start, z_own, z_oth, on_own, on_oth, high_ref, low_ref):
    rows, pairs, depth, lanes = z_oth.shape
    mine = pl.ds(start, depth)
    for g, (own, oth) in enumerate(((z_own, z_oth), (on_own, on_oth))):
        for i in range(rows):
            for j in range(pairs):
                at = ((g * rows + i) * pairs + j) * 2
                even, odd = unzip_lanes(own[i, j, mine], oth[i, j])
                high_ref[at], low_ref[at] = halves(even)
                high_ref[at + 1], low_ref[at + 1] = halves(odd)


def first_product(start, index_ref, near_high, near_low, off_own, off_oth, j_own_high, j_own_low, j_oth, *refs):
    p_ref, off_in, z_high, z_low, j_high, j_low, lhs_high, lhs_low, sems = refs
    rows, pairs, _, lanes = off_oth.shape
    depth = z_high.shape[1]
    mine = pl.ds(start, depth)
    half = j_oth.shape[2]
    slots = j_oth.shape[1]
    near = near_high.shape[0]
    copies = [
        pltpu.make_async_copy(src, dst, sems.at[n])
        for n, (src, dst) in enumerate((
            (off_own.at[:, :, mine], off_in),
            (near_high, z_high.at[pl.ds(0, near)]),
            (near_low, z_low.at[pl.ds(0, near)]),
            (j_own_high, j_high.at[:, pl.ds(0, half)]),
            (j_own_low, j_low.at[:, pl.ds(0, half)]),
        ))
    ]
    for copy in copies:
        copy.start()
    blank = z_high.shape[0] - 1
    z_high[blank] = jnp.zeros(z_high.shape[1:], jnp.bfloat16)
    z_low[blank] = jnp.zeros(z_low.shape[1:], jnp.bfloat16)
    for i in range(rows):
        for s in range(slots):
            place = (i, pl.ds(half, half), pl.ds(s * 128, 128))
            j_high[place], j_low[place] = halves(turn_lanes(j_oth[i, s]))
    copies[0].wait()
    for i in range(rows):
        for j in range(pairs):
            even, odd = unzip_lanes(off_in[i, j], off_oth[i, j])
            at = near + (i * pairs + j) * 2
            z_high[at], z_low[at] = halves(even)
            z_high[at + 1], z_low[at + 1] = halves(odd)
    for copy in copies[1:]:
        copy.wait()
    for i in range(rows):
        total = gather_dot(index_ref, i, slots, 2 * pairs, z_high, z_low, lhs_high, lhs_low,
                           (j_high[i], j_low[i]), ((1,), (1,)))
        p_ref[i] = total.reshape(2 * pairs, depth, lanes)


def left_blocks(chunks, z_own, z_rest, *refs):
    z_send, z_oth, (high_ref, low_ref) = refs[:chunks], refs[chunks : 2 * chunks], refs[2 * chunks :]
    rows, pairs, half, lanes = z_own.shape
    for i in range(rows):
        for j in range(pairs):
            oth = jnp.concatenate([ref[i, j] for ref in z_oth], axis=0)
            send = jnp.concatenate([ref[i, j] for ref in z_send], axis=0)
            for part, (x, y) in enumerate(((z_own[i, j], oth), (send, z_rest[i, j]))):
                for slot, block in enumerate(unzip_lanes(x, y)):
                    place = (i, pl.ds((2 * j + slot) * lanes + part * half, half))
                    high_ref[place], low_ref[place] = halves(block)


def second_product(index_ref, p_own, p_on, p_off, l_high, l_low, own_ref, send_ref,
                   p_high, p_low, lhs_high, lhs_low):
    rows, slots, depth, lanes = p_own.shape
    blank = p_high.shape[0] - 1
    p_high[blank] = jnp.zeros(p_high.shape[1:], jnp.bfloat16)
    p_low[blank] = jnp.zeros(p_low.shape[1:], jnp.bfloat16)
    for g, source in enumerate((p_own, p_on, p_off)):
        for i in range(rows):
            for k in range(slots):
                at = (g * rows + i) * slots + k
                p_high[at], p_low[at] = halves(source[i, k])
    for i in range(rows):
        total = gather_dot(index_ref, i, slots, slots, p_high, p_low, lhs_high, lhs_low,
                           (l_high[i], l_low[i]), ((1,), (0,)))
        total = total.reshape(slots, depth, lanes)
        for j in range(slots // 2):
            own_ref[i, j], send_ref[i, j] = unzip_lanes(total[2 * j], total[2 * j + 1])


def finish(chunks, z_ref, *refs):
    second = lax.axis_index("inner") == 1
    own, oth, (out_ref, staged, sems) = refs[:chunks], refs[chunks : 2 * chunks], refs[2 * chunks :]
    rows, slots, half, lanes = z_ref.shape
    copies = []
    for i in range(rows):
        for j in range(slots // 2):
            stack = jnp.concatenate([ref[i, j] for ref in own + oth], axis=0)
            turned = stack.T
            turned = jnp.where(second, swapped(turned), turned)
            staged[i, 2 * j : 2 * j + 2] = (
                2.0 * z_ref[i, 2 * j : 2 * j + 2] - turned.reshape(2, half, lanes)
            )
        copies.append(pltpu.make_async_copy(staged.at[i], out_ref.at[i], sems.at[i]))
        copies[-1].start()
    for copy in copies:
        copy.wait()


def half_shards(hardness_blocks, inverse_blocks, hardness_pattern, inverse_pattern):
    rows, slots, half, lanes = inverse_blocks.shape
    left_slots = hardness_blocks.shape[1]
    pairs = slots // 2
    count = lax.axis_size("rows")
    f32 = functools.partial(jax.ShapeDtypeStruct, dtype=jnp.float32)
    bf16 = functools.partial(jax.ShapeDtypeStruct, dtype=jnp.bfloat16)
    pack = f32((rows, pairs, half, lanes))
    smem = pl.BlockSpec(memory_space=pltpu.SMEM)
    vmem = pl.BlockSpec(memory_space=pltpu.VMEM)
    hbm = pl.BlockSpec(memory_space=pltpu.HBM)
    anywhere = pl.BlockSpec(memory_space=pl.ANY)

    def across(x):
        return lax.ppermute(x, "inner", [(0, 1), (1, 0)])

    def on_swap(x):
        return lax.ppermute(x, "rows", [(i, i ^ 1) for i in range(count)])

    def off_swap(x):
        inside = [(i, i + 1) for i in range(1, count - 1, 2)]
        return lax.ppermute(x, "rows", inside + [(b, a) for a, b in inside])

    find = call(
        find_blocks,
        (
            jax.ShapeDtypeStruct((rows * left_slots * slots,), jnp.int32),
            jax.ShapeDtypeStruct((rows * slots * slots,), jnp.int32),
        ),
        "find_blocks",
        scratch=[pltpu.SMEM((3 * rows * (2 * REACH + 1),), jnp.int32)],
        specs=[smem, smem],
        out_specs=[smem, smem],
    )
    take_rows = call(left_rows, (bf16((rows, half, left_slots * lanes)),) * 2, "left_rows")
    chunks = [f32((rows, pairs, depth, lanes)) for depth in CHUNKS]
    z_send = call(functools.partial(split_columns, True), tuple(chunks), "split_send")(inverse_blocks)
    z_own = call(functools.partial(split_columns, False), pack, "split_own", specs=[vmem, anywhere])(
        inverse_blocks, z_send[0]
    )
    z_oth = [across(x) for x in z_send]
    off_own = off_swap(z_own)
    z_send = list(z_send)
    on_own = on_swap(z_own)
    after = lax.optimization_barrier
    inverse_pattern, z_own = after((inverse_pattern, z_own))
    flat_one, flat_two = find(hardness_pattern, inverse_pattern)
    z_oth[1], flat_one = after((z_oth[1], flat_one))
    later, flat_one = after((hardness_blocks, flat_one))
    j_oth = across(later)
    off_oth = [off_swap(x) for x in z_oth]
    on_oth = [on_swap(x) for x in z_oth]
    later, z_oth[1] = after((z_own, z_oth[1]))
    z_rest = across(later)
    later, off_own = after((hardness_blocks, off_own))
    j_own = list(take_rows(later))
    left = call(
        functools.partial(left_blocks, len(CHUNKS)), (bf16((rows, slots * lanes, lanes)),) * 2, "left_blocks"
    )(z_own, z_rest, *z_send, *z_oth)

    blocks = 3 * rows * slots + 1
    bf16_buffer = functools.partial(pltpu.VMEM, dtype=jnp.bfloat16)

    def first(start, depth, z_oth, off_oth, on_oth):
        near = call(
            functools.partial(merge_near, start), (bf16((2 * rows * slots, depth, lanes)),) * 2, "merge_near"
        )(z_own, z_oth, on_own, on_oth)
        return call(
            functools.partial(first_product, start),
            f32((rows, slots, depth, lanes)),
            "first_product",
            scratch=[pltpu.VMEM((rows, pairs, depth, lanes), jnp.float32)]
            + [bf16_buffer((blocks, depth, lanes))] * 2
            + [bf16_buffer((rows, lanes, left_slots * lanes))] * 2
            + [bf16_buffer((slots * depth, left_slots * lanes))] * 2
            + [pltpu.SemaphoreType.DMA((5,))],
            specs=[smem, hbm, hbm, hbm, vmem, hbm, hbm, vmem],
            flops=6 * rows * left_slots * slots * depth * lanes * lanes,
            nbytes=16 << 18,
        )(flat_one, *near, off_own, off_oth, *j_own, j_oth)

    products = []
    start = 0
    for depth, *oth in zip(CHUNKS, z_oth, off_oth, on_oth):
        p = first(start, depth, *oth)
        products.append((p, off_swap(p), on_swap(p)))
        start += depth

    def second(p, p_off, p_on):
        depth = p.shape[2]
        return call(
            second_product,
            (f32((rows, pairs, depth, lanes)),) * 2,
            "second_product",
            scratch=[bf16_buffer((blocks, depth, lanes))] * 2
            + [bf16_buffer((slots * depth, slots * lanes))] * 2,
            specs=[smem] + [vmem] * 5,
            flops=6 * rows * slots * slots * depth * lanes * lanes,
            nbytes=16 << 18,
        )(flat_two, p, p_on, p_off, *left)

    own, oth = [], []
    for p, p_off, p_on in products:
        mine, send = second(p, p_off, p_on)
        own.append(mine)
        oth.append(across(send))
    return call(
        functools.partial(finish, len(CHUNKS)),
        f32(inverse_blocks.shape),
        "finish",
        scratch=[pltpu.VMEM(inverse_blocks.shape, jnp.float32), pltpu.SemaphoreType.DMA((rows,))],
        specs=[vmem] * (1 + 2 * len(CHUNKS)),
        out_specs=anywhere,
        nbytes=12 << 18,
    )(inverse_blocks, *own, *oth)


def solution(mesh):
    in_specs = (
        P("rows", None, "inner", None),
        P("rows", None, "inner", None),
        P("rows", None),
        P(),
    )
    out_specs = P("rows", None, "inner", None)
    halved = mesh.shape["inner"] == 2 and mesh.shape["rows"] % 2 == 0
    shards = half_shards if halved else general_shards
    return jax.shard_map(shards, mesh=mesh, in_specs=in_specs, out_specs=out_specs, check_vma=False)
```

```python
import functools

import jax
import jax.numpy as jnp
from jax import lax
from jax.experimental import pallas as pl
from jax.experimental.pallas import tpu as pltpu
from jax.sharding import PartitionSpec as P

REACH = 5
PARTS = ((32,), (32,))
CHUNKS = tuple(sum(parts) for parts in PARTS)
VMEM_BYTES = 14 * 1024 * 1024


def with_halo(cells, sides, width):
    for axis, dim in sides:
        count = lax.axis_size(axis)
        ends = count - 1
        head = lax.slice_in_dim(cells, 0, width, axis=dim)
        tail = lax.slice_in_dim(cells, cells.shape[dim] - width, cells.shape[dim], axis=dim)
        cells = jnp.concatenate(
            [
                lax.ppermute(tail, axis, [(i, (i + 1) % count) for i in range(ends)]),
                cells,
                lax.ppermute(head, axis, [((i + 1) % count, i) for i in range(ends)]),
            ],
            axis=dim,
        )
    return cells


def match_slots(left_pattern, target_pattern, right_pattern, base):
    local = left_pattern - base
    listed = jnp.take(right_pattern, local, axis=0)
    equal = listed[:, :, None, :] == target_pattern[:, None, :, None]
    width = right_pattern.shape[1]
    slot = jnp.sum(jnp.where(equal, jnp.arange(width, dtype=jnp.int32), 0), axis=3)
    return local[:, :, None], slot, jnp.any(equal, axis=3)


def locate_blocks(left_pattern, target_pattern, right_pattern, base):
    local, slot, found = match_slots(left_pattern, target_pattern, right_pattern, base)
    width = right_pattern.shape[1]
    return jnp.where(found, local * width + slot, right_pattern.shape[0] * width)


def make_fold(left, flat, total, piece):
    count = piece.shape[2]
    lined = piece.reshape(piece.shape[0] * piece.shape[1], count, piece.shape[3])
    lined = jnp.concatenate([lined, jnp.zeros((1, count, piece.shape[3]), lined.dtype)], axis=0)
    for slot in range(flat.shape[1]):
        chosen = jnp.take(lined, flat[:, slot].reshape(-1), axis=0)
        chosen = chosen.reshape(flat.shape[0], flat.shape[2], count, piece.shape[3])
        total = total + jnp.einsum(
            "irp,ikpd->ikrd", left[:, slot], chosen, precision=lax.Precision.HIGHEST
        )
    return total


def patterns_beside(inverse_pattern, count_rows):
    first_row = lax.axis_index("rows") * count_rows
    padded = jnp.pad(inverse_pattern, ((REACH, REACH), (0, 0)), constant_values=-1)
    beside_all = lax.dynamic_slice_in_dim(padded, first_row, count_rows + 2 * REACH, 0)
    own_pattern = lax.dynamic_slice_in_dim(inverse_pattern, first_row, count_rows, 0)
    return first_row - REACH, beside_all, own_pattern


def general_shards(hardness_blocks, inverse_blocks, hardness_pattern, inverse_pattern):
    count_rows = inverse_blocks.shape[0]
    base, beside_all, own_pattern = patterns_beside(inverse_pattern, count_rows)
    flat_one = locate_blocks(hardness_pattern, own_pattern, beside_all, base)
    flat_two = locate_blocks(own_pattern, own_pattern, beside_all, base)
    empty = jnp.zeros(
        (count_rows, own_pattern.shape[1], inverse_blocks.shape[2], inverse_blocks.shape[3]),
        jnp.float32,
    )
    extended = with_halo(inverse_blocks, (("rows", 0),), REACH)
    product = make_fold(
        hardness_blocks, flat_one, empty, lax.all_gather(extended, "inner", axis=2, tiled=True)
    )
    product_ext = with_halo(product, (("rows", 0),), REACH)
    carried = make_fold(
        inverse_blocks, flat_two, empty, lax.all_gather(product_ext, "inner", axis=2, tiled=True)
    )
    return 2.0 * inverse_blocks - carried


def call(body, outs, name, scratch=(), specs=None, out_specs=None, flops=0, nbytes=0):
    params = dict(
        out_shape=outs,
        scratch_shapes=list(scratch),
        compiler_params=pltpu.CompilerParams(vmem_limit_bytes=VMEM_BYTES),
        name=name,
        cost_estimate=pl.CostEstimate(flops=flops, bytes_accessed=nbytes, transcendentals=0),
    )
    if specs is not None:
        params.update(in_specs=specs)
    if out_specs is not None:
        params.update(out_specs=out_specs)
    return pl.pallas_call(body, **params)


def is_low(shape):
    return lax.broadcasted_iota(jnp.int32, shape, len(shape) - 1) < shape[-1] // 2


def swapped(x):
    return pltpu.roll(x, x.shape[-1] // 2, x.ndim - 1)


def unzip_lanes(a, b):
    low = is_low(a.shape)
    return jnp.where(low, a, swapped(b)), jnp.where(low, swapped(a), b)


def halves(x):
    high = x.astype(jnp.bfloat16)
    return high, (x - high.astype(jnp.float32)).astype(jnp.bfloat16)


def find_blocks(left_ref, pattern_ref, one_ref, two_ref, table):
    rows = left_ref.shape[0]
    slots = pattern_ref.shape[1]
    device = lax.axis_index("rows")
    first = device * rows
    last = pattern_ref.shape[0] - 1
    odd = device % 2
    width = 2 * REACH + 1
    none = 3 * rows * slots

    @pl.loop(0, 3 * rows)
    def _(n):
        for shift in range(width):
            table[n * width + shift] = none

    for n, segment in enumerate((2 - odd, 0, 1 + odd)):

        @pl.loop(0, rows)
        def _(r):
            local = n * rows + r
            row = jnp.clip(first + local - rows, 0, last)
            shifts = [pattern_ref[row, k] - row + REACH for k in range(slots)]
            for k, shift in enumerate(shifts):
                table[local * width + shift] = (segment * rows + r) * slots + k

    @pl.loop(0, rows)
    def _(i):
        columns = [pattern_ref[first + i, k] for k in range(slots)]
        for count, lefts, out_ref in (
            (left_ref.shape[1], [left_ref[i, s] for s in range(left_ref.shape[1])], one_ref),
            (slots, columns, two_ref),
        ):
            found = []
            for row in lefts:
                at = (row - first + rows) * width
                for column in columns:
                    shift = column - row + REACH
                    inside = (shift >= 0) & (shift < width)
                    found.append(jnp.where(inside, table[at + jnp.clip(shift, 0, width - 1)], none))
            for n, value in enumerate(found):
                out_ref[i * count * slots + n] = value


def split_columns(send, z_ref, *refs):
    out_refs = refs[0 if send else 1 :]
    second = lax.axis_index("inner") == 1
    rows, slots, half, lanes = z_ref.shape
    for i in range(rows):
        for j in range(slots // 2):
            turned = z_ref[i, 2 * j : 2 * j + 2].reshape(2 * half, lanes).T
            top, bottom = turned[:half], turned[half:]
            part = jnp.where(second, top, bottom) if send else jnp.where(second, bottom, top)
            start = 0
            for out_ref in out_refs:
                depth = out_ref.shape[2]
                out_ref[i, j] = part[start : start + depth]
                start += depth


def gather_dot(index_ref, i, right_slots, out_slots, high_ref, low_ref, lhs_high, lhs_low, right, dims):
    depth = high_ref.shape[1]
    for s in range(right_slots):
        for k in range(out_slots):
            at = index_ref[(i * right_slots + s) * out_slots + k]
            place = (pl.ds(k * depth, depth), pl.ds(s * 128, 128))
            lhs_high[place] = high_ref[at]
            lhs_low[place] = low_ref[at]
    dot = functools.partial(
        lax.dot_general, dimension_numbers=(dims, ((), ())), preferred_element_type=jnp.float32
    )
    both, high = right
    total = dot(lhs_high[...], both)
    count = total.shape[1] // 2
    return total[:, :count] + (total[:, count:] + dot(lhs_low[...], high))


def turn_lanes(x):
    return jnp.where(lax.axis_index("inner") == 1, swapped(x), x)


def left_rows(j_ref, high_ref, low_ref):
    for i in range(j_ref.shape[0]):
        for s in range(j_ref.shape[1]):
            place = (i, slice(None), pl.ds(s * 128, 128))
            high_ref[place], low_ref[place] = halves(turn_lanes(j_ref[i, s]))


def merge_near(start, z_own, z_oth, on_own, on_oth, high_ref, low_ref):
    rows, pairs, depth, lanes = z_oth.shape
    mine = pl.ds(start, depth)
    for g, (own, oth) in enumerate(((z_own, z_oth), (on_own, on_oth))):
        for i in range(rows):
            for j in range(pairs):
                at = ((g * rows + i) * pairs + j) * 2
                even, odd = unzip_lanes(own[i, j, mine], oth[i, j])
                high_ref[at], low_ref[at] = halves(even)
                high_ref[at + 1], low_ref[at + 1] = halves(odd)


def first_product(start, index_ref, near_high, near_low, off_own, off_oth, j_own_high, j_own_low, j_oth, *refs):
    *p_refs, off_in, z_high, z_low, j_both, lhs_high, lhs_low, sems = refs
    rows, pairs, _, lanes = off_oth.shape
    depth = z_high.shape[1]
    mine = pl.ds(start, depth)
    half = j_oth.shape[2]
    slots = j_oth.shape[1]
    near = near_high.shape[0]
    copy = pltpu.make_async_copy(off_own.at[:, :, mine], off_in, sems.at[0])
    copy.start()
    z_high[:near], z_low[:near] = near_high[...], near_low[...]
    j_both[:, :half], j_both[:, 2 * half : 3 * half] = j_own_high[...], j_own_low[...]
    blank = z_high.shape[0] - 1
    z_high[blank] = jnp.zeros(z_high.shape[1:], jnp.bfloat16)
    z_low[blank] = jnp.zeros(z_low.shape[1:], jnp.bfloat16)
    for i in range(rows):
        for s in range(slots):
            place = pl.ds(s * 128, 128)
            j_both[i, half : 2 * half, place], j_both[i, 3 * half :, place] = halves(turn_lanes(j_oth[i, s]))
    copy.wait()
    for i in range(rows):
        for j in range(pairs):
            even, odd = unzip_lanes(off_in[i, j], off_oth[i, j])
            at = near + (i * pairs + j) * 2
            z_high[at], z_low[at] = halves(even)
            z_high[at + 1], z_low[at + 1] = halves(odd)
    for i in range(rows):
        total = gather_dot(index_ref, i, slots, 2 * pairs, z_high, z_low, lhs_high, lhs_low,
                           (j_both[i], j_both[i, : 2 * half]), ((1,), (1,)))
        total = total.reshape(2 * pairs, depth, lanes)
        at = 0
        for p_ref in p_refs:
            count = p_ref.shape[2]
            p_ref[i] = total[:, at : at + count]
            at += count


def left_blocks(chunks, z_own, z_rest, *refs):
    z_send, z_oth, both_ref = refs[:chunks], refs[chunks : 2 * chunks], refs[-1]
    rows, pairs, half, lanes = z_own.shape
    for i in range(rows):
        for j in range(pairs):
            oth = jnp.concatenate([ref[i, j] for ref in z_oth], axis=0)
            send = jnp.concatenate([ref[i, j] for ref in z_send], axis=0)
            for part, (x, y) in enumerate(((z_own[i, j], oth), (send, z_rest[i, j]))):
                for slot, block in enumerate(unzip_lanes(x, y)):
                    place = pl.ds((2 * j + slot) * lanes + part * half, half)
                    both_ref[i, place, :lanes], both_ref[i, place, lanes:] = halves(block)


def second_product(index_ref, p_own, p_on, p_off, l_both, own_ref, send_ref,
                   p_high, p_low, lhs_high, lhs_low):
    rows, slots, depth, lanes = p_own.shape
    blank = p_high.shape[0] - 1
    p_high[blank] = jnp.zeros(p_high.shape[1:], jnp.bfloat16)
    p_low[blank] = jnp.zeros(p_low.shape[1:], jnp.bfloat16)
    for g, source in enumerate((p_own, p_on, p_off)):
        for i in range(rows):
            for k in range(slots):
                at = (g * rows + i) * slots + k
                p_high[at], p_low[at] = halves(source[i, k])
    for i in range(rows):
        total = gather_dot(index_ref, i, slots, slots, p_high, p_low, lhs_high, lhs_low,
                           (l_both[i], l_both[i, :, :128]), ((1,), (0,)))
        total = total.reshape(slots, depth, lanes)
        for j in range(slots // 2):
            own_ref[i, j], send_ref[i, j] = unzip_lanes(total[2 * j], total[2 * j + 1])


def finish(chunks, z_ref, *refs):
    second = lax.axis_index("inner") == 1
    own, oth, (out_ref, staged, sems) = refs[:chunks], refs[chunks : 2 * chunks], refs[2 * chunks :]
    rows, slots, half, lanes = z_ref.shape
    copies = []
    for i in range(rows):
        for j in range(slots // 2):
            stack = jnp.concatenate([ref[i, j] for ref in own + oth], axis=0)
            turned = stack.T
            turned = jnp.where(second, swapped(turned), turned)
            staged[i, 2 * j : 2 * j + 2] = (
                2.0 * z_ref[i, 2 * j : 2 * j + 2] - turned.reshape(2, half, lanes)
            )
        copies.append(pltpu.make_async_copy(staged.at[i], out_ref.at[i], sems.at[i]))
        copies[-1].start()
    for copy in copies:
        copy.wait()


def half_shards(hardness_blocks, inverse_blocks, hardness_pattern, inverse_pattern):
    rows, slots, half, lanes = inverse_blocks.shape
    left_slots = hardness_blocks.shape[1]
    pairs = slots // 2
    count = lax.axis_size("rows")
    f32 = functools.partial(jax.ShapeDtypeStruct, dtype=jnp.float32)
    bf16 = functools.partial(jax.ShapeDtypeStruct, dtype=jnp.bfloat16)
    pack = f32((rows, pairs, half, lanes))
    smem = pl.BlockSpec(memory_space=pltpu.SMEM)
    vmem = pl.BlockSpec(memory_space=pltpu.VMEM)
    hbm = pl.BlockSpec(memory_space=pltpu.HBM)
    anywhere = pl.BlockSpec(memory_space=pl.ANY)

    def across(x):
        return lax.ppermute(x, "inner", [(0, 1), (1, 0)])

    def on_swap(x):
        return lax.ppermute(x, "rows", [(i, i ^ 1) for i in range(count)])

    def off_swap(x):
        inside = [(i, i + 1) for i in range(1, count - 1, 2)]
        return lax.ppermute(x, "rows", inside + [(b, a) for a, b in inside])

    find = call(
        find_blocks,
        (
            jax.ShapeDtypeStruct((rows * left_slots * slots,), jnp.int32),
            jax.ShapeDtypeStruct((rows * slots * slots,), jnp.int32),
        ),
        "find_blocks",
        scratch=[pltpu.SMEM((3 * rows * (2 * REACH + 1),), jnp.int32)],
        specs=[smem, smem],
        out_specs=[smem, smem],
    )
    take_rows = call(left_rows, (bf16((rows, half, left_slots * lanes)),) * 2, "left_rows")
    chunks = [f32((rows, pairs, depth, lanes)) for depth in CHUNKS]
    z_send = call(functools.partial(split_columns, True), tuple(chunks), "split_send")(inverse_blocks)
    z_own = call(functools.partial(split_columns, False), pack, "split_own", specs=[vmem, anywhere])(
        inverse_blocks, z_send[0]
    )
    z_oth = [across(x) for x in z_send]
    off_own = off_swap(z_own)
    z_send = list(z_send)
    on_own = on_swap(z_own)
    after = lax.optimization_barrier
    inverse_pattern, z_own = after((inverse_pattern, z_own))
    flat_one, flat_two = find(hardness_pattern, inverse_pattern)
    z_oth[1], flat_one = after((z_oth[1], flat_one))
    later, flat_one = after((hardness_blocks, flat_one))
    j_oth = across(later)
    off_oth = [off_swap(x) for x in z_oth]
    on_oth = [on_swap(x) for x in z_oth]
    later, z_oth[1] = after((z_own, z_oth[1]))
    z_rest = across(later)
    later, off_own = after((hardness_blocks, off_own))
    j_own = list(take_rows(later))
    left = call(
        functools.partial(left_blocks, len(CHUNKS)), bf16((rows, slots * lanes, 2 * lanes)), "left_blocks"
    )(z_own, z_rest, *z_send, *z_oth)

    blocks = 3 * rows * slots + 1
    bf16_buffer = functools.partial(pltpu.VMEM, dtype=jnp.bfloat16)

    def first(start, parts, z_oth, off_oth, on_oth):
        depth = sum(parts)
        near = call(
            functools.partial(merge_near, start), (bf16((2 * rows * slots, depth, lanes)),) * 2, "merge_near"
        )(z_own, z_oth, on_own, on_oth)
        return call(
            functools.partial(first_product, start),
            tuple(f32((rows, slots, part, lanes)) for part in parts),
            "first_product",
            scratch=[pltpu.VMEM((rows, pairs, depth, lanes), jnp.float32)]
            + [bf16_buffer((blocks, depth, lanes))] * 2
            + [bf16_buffer((rows, 2 * lanes, left_slots * lanes))]
            + [bf16_buffer((slots * depth, left_slots * lanes))] * 2
            + [pltpu.SemaphoreType.DMA((1,))],
            specs=[smem, vmem, vmem, hbm, vmem, vmem, vmem, vmem],
            flops=6 * rows * left_slots * slots * depth * lanes * lanes,
            nbytes=16 << 18,
        )(flat_one, *near, off_own, off_oth, *j_own, j_oth)

    products = []
    start = 0
    for parts, *oth in zip(PARTS, z_oth, off_oth, on_oth):
        products += [(p, off_swap(p), on_swap(p)) for p in first(start, parts, *oth)]
        start += sum(parts)

    def second(p, p_off, p_on):
        depth = p.shape[2]
        return call(
            second_product,
            (f32((rows, pairs, depth, lanes)),) * 2,
            "second_product",
            scratch=[bf16_buffer((blocks, depth, lanes))] * 2
            + [bf16_buffer((slots * depth, slots * lanes))] * 2,
            specs=[smem] + [vmem] * 4,
            flops=6 * rows * slots * slots * depth * lanes * lanes,
            nbytes=16 << 18,
        )(flat_two, p, p_on, p_off, left)

    own, oth = [], []
    for p, p_off, p_on in products:
        mine, send = second(p, p_off, p_on)
        own.append(mine)
        oth.append(across(send))
    return call(
        functools.partial(finish, len(products)),
        f32(inverse_blocks.shape),
        "finish",
        scratch=[pltpu.VMEM(inverse_blocks.shape, jnp.float32), pltpu.SemaphoreType.DMA((rows,))],
        specs=[vmem] * (1 + 2 * len(products)),
        out_specs=anywhere,
        nbytes=12 << 18,
    )(inverse_blocks, *own, *oth)


def solution(mesh):
    in_specs = (
        P("rows", None, "inner", None),
        P("rows", None, "inner", None),
        P("rows", None),
        P(),
    )
    out_specs = P("rows", None, "inner", None)
    halved = mesh.shape["inner"] == 2 and mesh.shape["rows"] % 2 == 0
    shards = half_shards if halved else general_shards
    return jax.shard_map(shards, mesh=mesh, in_specs=in_specs, out_specs=out_specs, check_vma=False)
```

```python
import functools

import jax
import jax.numpy as jnp
from jax import lax
from jax.experimental import pallas as pl
from jax.experimental.pallas import tpu as pltpu
from jax.sharding import PartitionSpec as P

REACH = 5
CHUNKS = (32, 32)
VMEM_BYTES = 14 * 1024 * 1024


def with_halo(cells, sides, width):
    for axis, dim in sides:
        count = lax.axis_size(axis)
        ends = count - 1
        head = lax.slice_in_dim(cells, 0, width, axis=dim)
        tail = lax.slice_in_dim(cells, cells.shape[dim] - width, cells.shape[dim], axis=dim)
        cells = jnp.concatenate(
            [
                lax.ppermute(tail, axis, [(i, (i + 1) % count) for i in range(ends)]),
                cells,
                lax.ppermute(head, axis, [((i + 1) % count, i) for i in range(ends)]),
            ],
            axis=dim,
        )
    return cells


def match_slots(left_pattern, target_pattern, right_pattern, base):
    local = left_pattern - base
    listed = jnp.take(right_pattern, local, axis=0)
    equal = listed[:, :, None, :] == target_pattern[:, None, :, None]
    width = right_pattern.shape[1]
    slot = jnp.sum(jnp.where(equal, jnp.arange(width, dtype=jnp.int32), 0), axis=3)
    return local[:, :, None], slot, jnp.any(equal, axis=3)


def locate_blocks(left_pattern, target_pattern, right_pattern, base):
    local, slot, found = match_slots(left_pattern, target_pattern, right_pattern, base)
    width = right_pattern.shape[1]
    return jnp.where(found, local * width + slot, right_pattern.shape[0] * width)


def make_fold(left, flat, total, piece):
    count = piece.shape[2]
    lined = piece.reshape(piece.shape[0] * piece.shape[1], count, piece.shape[3])
    lined = jnp.concatenate([lined, jnp.zeros((1, count, piece.shape[3]), lined.dtype)], axis=0)
    for slot in range(flat.shape[1]):
        chosen = jnp.take(lined, flat[:, slot].reshape(-1), axis=0)
        chosen = chosen.reshape(flat.shape[0], flat.shape[2], count, piece.shape[3])
        total = total + jnp.einsum(
            "irp,ikpd->ikrd", left[:, slot], chosen, precision=lax.Precision.HIGHEST
        )
    return total


def patterns_beside(inverse_pattern, count_rows):
    first_row = lax.axis_index("rows") * count_rows
    padded = jnp.pad(inverse_pattern, ((REACH, REACH), (0, 0)), constant_values=-1)
    beside_all = lax.dynamic_slice_in_dim(padded, first_row, count_rows + 2 * REACH, 0)
    own_pattern = lax.dynamic_slice_in_dim(inverse_pattern, first_row, count_rows, 0)
    return first_row - REACH, beside_all, own_pattern


def general_shards(hardness_blocks, inverse_blocks, hardness_pattern, inverse_pattern):
    count_rows = inverse_blocks.shape[0]
    base, beside_all, own_pattern = patterns_beside(inverse_pattern, count_rows)
    flat_one = locate_blocks(hardness_pattern, own_pattern, beside_all, base)
    flat_two = locate_blocks(own_pattern, own_pattern, beside_all, base)
    empty = jnp.zeros(
        (count_rows, own_pattern.shape[1], inverse_blocks.shape[2], inverse_blocks.shape[3]),
        jnp.float32,
    )
    extended = with_halo(inverse_blocks, (("rows", 0),), REACH)
    product = make_fold(
        hardness_blocks, flat_one, empty, lax.all_gather(extended, "inner", axis=2, tiled=True)
    )
    product_ext = with_halo(product, (("rows", 0),), REACH)
    carried = make_fold(
        inverse_blocks, flat_two, empty, lax.all_gather(product_ext, "inner", axis=2, tiled=True)
    )
    return 2.0 * inverse_blocks - carried


def call(body, outs, name, scratch=(), specs=None, out_specs=None, flops=0, nbytes=0):
    params = dict(
        out_shape=outs,
        scratch_shapes=list(scratch),
        compiler_params=pltpu.CompilerParams(vmem_limit_bytes=VMEM_BYTES),
        name=name,
        cost_estimate=pl.CostEstimate(flops=flops, bytes_accessed=nbytes, transcendentals=0),
    )
    if specs is not None:
        params.update(in_specs=specs)
    if out_specs is not None:
        params.update(out_specs=out_specs)
    return pl.pallas_call(body, **params)


def is_low(shape):
    return lax.broadcasted_iota(jnp.int32, shape, len(shape) - 1) < shape[-1] // 2


def swapped(x):
    return pltpu.roll(x, x.shape[-1] // 2, x.ndim - 1)


def unzip_lanes(a, b):
    low = is_low(a.shape)
    return jnp.where(low, a, swapped(b)), jnp.where(low, swapped(a), b)


def halves(x):
    high = x.astype(jnp.bfloat16)
    return high, (x - high.astype(jnp.float32)).astype(jnp.bfloat16)


def find_blocks(left_ref, pattern_ref, one_ref, two_ref, table):
    rows = left_ref.shape[0]
    slots = pattern_ref.shape[1]
    device = lax.axis_index("rows")
    first = device * rows
    last = pattern_ref.shape[0] - 1
    odd = device % 2
    width = 2 * REACH + 1
    none = 3 * rows * slots

    @pl.loop(0, 3 * rows)
    def _(n):
        for shift in range(width):
            table[n * width + shift] = none

    for n, segment in enumerate((2 - odd, 0, 1 + odd)):

        @pl.loop(0, rows)
        def _(r):
            local = n * rows + r
            row = jnp.clip(first + local - rows, 0, last)
            shifts = [pattern_ref[row, k] - row + REACH for k in range(slots)]
            for k, shift in enumerate(shifts):
                table[local * width + shift] = (segment * rows + r) * slots + k

    @pl.loop(0, rows)
    def _(i):
        columns = [pattern_ref[first + i, k] for k in range(slots)]
        for count, lefts, out_ref in (
            (left_ref.shape[1], [left_ref[i, s] for s in range(left_ref.shape[1])], one_ref),
            (slots, columns, two_ref),
        ):
            found = []
            for row in lefts:
                at = (row - first + rows) * width
                for column in columns:
                    shift = column - row + REACH
                    inside = (shift >= 0) & (shift < width)
                    found.append(jnp.where(inside, table[at + jnp.clip(shift, 0, width - 1)], none))
            for n, value in enumerate(found):
                out_ref[i * count * slots + n] = value


def split_columns(send, z_ref, *refs):
    out_refs = refs[0 if send else 1 :]
    second = lax.axis_index("inner") == 1
    rows, slots, half, lanes = z_ref.shape
    for i in range(rows):
        for j in range(slots // 2):
            turned = z_ref[i, 2 * j : 2 * j + 2].reshape(2 * half, lanes).T
            top, bottom = turned[:half], turned[half:]
            part = jnp.where(second, top, bottom) if send else jnp.where(second, bottom, top)
            start = 0
            for out_ref in out_refs:
                depth = out_ref.shape[2]
                out_ref[i, j] = part[start : start + depth]
                start += depth


def gather_dot(index_ref, i, right_slots, out_slots, high_ref, low_ref, lhs_high, lhs_low, right, dims):
    depth = high_ref.shape[1]
    for s in range(right_slots):
        for k in range(out_slots):
            at = index_ref[(i * right_slots + s) * out_slots + k]
            place = (pl.ds(k * depth, depth), pl.ds(s * 128, 128))
            lhs_high[place] = high_ref[at]
            lhs_low[place] = low_ref[at]
    dot = functools.partial(
        lax.dot_general, dimension_numbers=(dims, ((), ())), preferred_element_type=jnp.float32
    )
    both, high = right
    total = dot(lhs_high[...], both)
    count = total.shape[1] // 2
    return total[:, :count] + (total[:, count:] + dot(lhs_low[...], high))


def turn_lanes(x):
    return jnp.where(lax.axis_index("inner") == 1, swapped(x), x)


def left_rows(j_ref, high_ref, low_ref):
    for i in range(j_ref.shape[0]):
        for s in range(j_ref.shape[1]):
            place = (i, slice(None), pl.ds(s * 128, 128))
            high_ref[place], low_ref[place] = halves(turn_lanes(j_ref[i, s]))


def merge_near(start, z_own, z_oth, on_own, on_oth, high_ref, low_ref):
    rows, pairs, depth, lanes = z_oth.shape
    mine = pl.ds(start, depth)
    for g, (own, oth) in enumerate(((z_own, z_oth), (on_own, on_oth))):
        for i in range(rows):
            for j in range(pairs):
                at = ((g * rows + i) * pairs + j) * 2
                even, odd = unzip_lanes(own[i, j, mine], oth[i, j])
                high_ref[at], low_ref[at] = halves(even)
                high_ref[at + 1], low_ref[at + 1] = halves(odd)


def take_blocks(start, near_high, near_low, off_own, off_oth, off_in, z_high, z_low, sem):
    rows, pairs, depth, lanes = off_oth.shape
    near = near_high.shape[0]
    copy = pltpu.make_async_copy(off_own.at[:, :, pl.ds(start, depth)], off_in, sem)
    copy.start()
    z_high[:near], z_low[:near] = near_high[...], near_low[...]
    blank = z_high.shape[0] - 1
    z_high[blank] = jnp.zeros(z_high.shape[1:], jnp.bfloat16)
    z_low[blank] = jnp.zeros(z_low.shape[1:], jnp.bfloat16)
    copy.wait()
    for i in range(rows):
        for j in range(pairs):
            even, odd = unzip_lanes(off_in[i, j], off_oth[i, j])
            at = near + (i * pairs + j) * 2
            z_high[at], z_low[at] = halves(even)
            z_high[at + 1], z_low[at + 1] = halves(odd)


def first_product(start, index_ref, near_high, near_low, off_own, off_oth, j_own_high, j_own_low,
                  j_oth_high, j_oth_low, p_ref, p_rest_ref, off_in, z_high, z_low, j_both, lhs_high, lhs_low,
                  sems):
    rows, pairs, depth, lanes = off_oth.shape
    half, slots = j_own_high.shape[1], j_own_high.shape[2] // 128
    for n, part in enumerate((j_own_high, j_oth_high, j_own_low, j_oth_low)):
        j_both[:, n * half : (n + 1) * half] = part[...]
    take_blocks(start, near_high, near_low, off_own, off_oth, off_in, z_high, z_low, sems.at[0])
    for i in range(rows):
        total = gather_dot(index_ref, i, slots, 2 * pairs, z_high, z_low, lhs_high, lhs_low,
                           (j_both[i], j_both[i, : 2 * half]), ((1,), (1,)))
        total = total.reshape(2 * pairs, depth, lanes)
        p_ref[i], p_rest_ref[i] = total[:pairs], total[pairs:]


def first_half_product(start, index_ref, near_high, near_low, off_own, off_oth, rows_high, rows_low,
                       p_ref, off_in, z_high, z_low, j_both, lhs_high, lhs_low, sems):
    rows, pairs, depth, lanes = off_oth.shape
    half, slots = rows_high.shape[1], rows_high.shape[2] // 128
    for n, part in enumerate((rows_high, rows_high, rows_low, rows_low)):
        j_both[:, n * half : (n + 1) * half] = part[...]
    take_blocks(start, near_high, near_low, off_own, off_oth, off_in, z_high, z_low, sems.at[0])
    for i in range(rows):
        total = gather_dot(index_ref, i, slots, 2 * pairs, z_high, z_low, lhs_high, lhs_low,
                           (j_both[i], j_both[i, : 2 * half]), ((1,), (1,)))
        total = total.reshape(2 * pairs, depth, lanes)
        for j in range(pairs):
            p_ref[i, j] = jnp.where(is_low((depth, lanes)), total[2 * j], total[2 * j + 1])


def left_blocks(chunks, z_own, z_rest, *refs):
    z_send, z_oth, both_ref = refs[:chunks], refs[chunks : 2 * chunks], refs[-1]
    rows, pairs, half, lanes = z_own.shape
    for i in range(rows):
        for j in range(pairs):
            oth = jnp.concatenate([ref[i, j] for ref in z_oth], axis=0)
            send = jnp.concatenate([ref[i, j] for ref in z_send], axis=0)
            for part, (x, y) in enumerate(((z_own[i, j], oth), (send, z_rest[i, j]))):
                for slot, block in enumerate(unzip_lanes(x, y)):
                    place = pl.ds((2 * j + slot) * lanes + part * half, half)
                    both_ref[i, place, :lanes], both_ref[i, place, lanes:] = halves(block)


def second_product(packed, index_ref, *refs):
    sources, (l_both, own_ref, send_ref, p_high, p_low, lhs_high, lhs_low) = refs[:6], refs[6:]
    rows, pairs, depth, lanes = own_ref.shape
    slots = 2 * pairs
    blank = p_high.shape[0] - 1
    p_high[blank] = jnp.zeros(p_high.shape[1:], jnp.bfloat16)
    p_low[blank] = jnp.zeros(p_low.shape[1:], jnp.bfloat16)
    for g in range(3):
        for i in range(rows):
            for j in range(pairs):
                blocks = sources[g][i, j], sources[3 + g][i, j]
                places = j, pairs + j
                if packed:
                    blocks = unzip_lanes(*blocks)
                    places = 2 * j, 2 * j + 1
                for slot, block in zip(places, blocks):
                    at = (g * rows + i) * slots + slot
                    p_high[at], p_low[at] = halves(block)
    for i in range(rows):
        total = gather_dot(index_ref, i, slots, slots, p_high, p_low, lhs_high, lhs_low,
                           (l_both[i], l_both[i, :, :128]), ((1,), (0,)))
        total = total.reshape(slots, depth, lanes)
        for j in range(pairs):
            own_ref[i, j], send_ref[i, j] = unzip_lanes(total[2 * j], total[2 * j + 1])


def finish(chunks, z_ref, *refs):
    second = lax.axis_index("inner") == 1
    own, oth, (out_ref, staged, sems) = refs[:chunks], refs[chunks : 2 * chunks], refs[2 * chunks :]
    rows, slots, half, lanes = z_ref.shape
    copies = []
    for i in range(rows):
        for j in range(slots // 2):
            stack = jnp.concatenate([ref[i, j] for ref in own + oth], axis=0)
            turned = stack.T
            turned = jnp.where(second, swapped(turned), turned)
            staged[i, 2 * j : 2 * j + 2] = (
                2.0 * z_ref[i, 2 * j : 2 * j + 2] - turned.reshape(2, half, lanes)
            )
        copies.append(pltpu.make_async_copy(staged.at[i], out_ref.at[i], sems.at[i]))
        copies[-1].start()
    for copy in copies:
        copy.wait()


def half_shards(hardness_blocks, inverse_blocks, hardness_pattern, inverse_pattern):
    rows, slots, half, lanes = inverse_blocks.shape
    left_slots = hardness_blocks.shape[1]
    pairs = slots // 2
    count = lax.axis_size("rows")
    f32 = functools.partial(jax.ShapeDtypeStruct, dtype=jnp.float32)
    bf16 = functools.partial(jax.ShapeDtypeStruct, dtype=jnp.bfloat16)
    pack = f32((rows, pairs, half, lanes))
    smem = pl.BlockSpec(memory_space=pltpu.SMEM)
    vmem = pl.BlockSpec(memory_space=pltpu.VMEM)
    hbm = pl.BlockSpec(memory_space=pltpu.HBM)
    anywhere = pl.BlockSpec(memory_space=pl.ANY)

    def across(x):
        return lax.ppermute(x, "inner", [(0, 1), (1, 0)])

    def on_swap(x):
        return lax.ppermute(x, "rows", [(i, i ^ 1) for i in range(count)])

    def off_swap(x):
        inside = [(i, i + 1) for i in range(1, count - 1, 2)]
        return lax.ppermute(x, "rows", inside + [(b, a) for a, b in inside])

    find = call(
        find_blocks,
        (
            jax.ShapeDtypeStruct((rows * left_slots * slots,), jnp.int32),
            jax.ShapeDtypeStruct((rows * slots * slots,), jnp.int32),
        ),
        "find_blocks",
        scratch=[pltpu.SMEM((3 * rows * (2 * REACH + 1),), jnp.int32)],
        specs=[smem, smem],
        out_specs=[smem, smem],
    )
    take_rows = call(left_rows, (bf16((rows, half, left_slots * lanes)),) * 2, "left_rows")
    chunks = [f32((rows, pairs, depth, lanes)) for depth in CHUNKS]
    z_send = call(functools.partial(split_columns, True), tuple(chunks), "split_send")(inverse_blocks)
    z_own = call(functools.partial(split_columns, False), pack, "split_own", specs=[vmem, anywhere])(
        inverse_blocks, z_send[0]
    )
    z_oth = [across(x) for x in z_send]
    off_own = off_swap(z_own)
    z_send = list(z_send)
    on_own = on_swap(z_own)
    after = lax.optimization_barrier
    inverse_pattern, z_own = after((inverse_pattern, z_own))
    flat_one, flat_two = find(hardness_pattern, inverse_pattern)
    z_oth[1], flat_one = after((z_oth[1], flat_one))
    later, flat_one = after((hardness_blocks, flat_one))
    j_oth = across(later)
    off_oth = [off_swap(x) for x in z_oth]
    on_oth = [on_swap(x) for x in z_oth]
    later, z_oth[1] = after((z_own, z_oth[1]))
    z_rest = across(later)
    later, off_own = after((hardness_blocks, off_own))
    j_own = list(take_rows(later))
    left = call(
        functools.partial(left_blocks, len(CHUNKS)), bf16((rows, slots * lanes, 2 * lanes)), "left_blocks"
    )(z_own, z_rest, *z_send, *z_oth)

    blocks = 3 * rows * slots + 1
    bf16_buffer = functools.partial(pltpu.VMEM, dtype=jnp.bfloat16)

    def beside(start, depth, z_oth, on_oth):
        return call(
            functools.partial(merge_near, start), (bf16((2 * rows * slots, depth, lanes)),) * 2, "merge_near"
        )(z_own, z_oth, on_own, on_oth)

    def first(body, name, count, start, depth, near, off_oth, j_rows):
        return call(
            functools.partial(body, start),
            (f32((rows, pairs, depth, lanes)),) * count,
            name,
            scratch=[pltpu.VMEM((rows, pairs, depth, lanes), jnp.float32)]
            + [bf16_buffer((blocks, depth, lanes))] * 2
            + [bf16_buffer((rows, 2 * lanes, left_slots * lanes))]
            + [bf16_buffer((slots * depth, left_slots * lanes))] * 2
            + [pltpu.SemaphoreType.DMA((1,))],
            specs=[smem, vmem, vmem, hbm, vmem] + [vmem] * len(j_rows),
        )(flat_one, *near, off_own, off_oth, *j_rows)

    def second(packed, depth, products):
        return call(
            functools.partial(second_product, packed),
            (f32((rows, pairs, depth, lanes)),) * 2,
            "second_product",
            scratch=[bf16_buffer((blocks, depth, lanes))] * 2
            + [bf16_buffer((slots * depth, slots * lanes))] * 2,
            specs=[smem] + [vmem] * 7,
        )(flat_two, *products, left)

    depth_one, depth_two = CHUNKS
    near = beside(0, depth_one, z_oth[0], on_oth[0])
    (one,) = first(first_half_product, "first_half_product", 1, 0, depth_one, near, off_oth[0], j_own)
    one_on, one_off = on_swap(one), off_swap(one)
    j_other = take_rows(j_oth)
    (two,) = first(first_half_product, "first_half_product", 1, 0, depth_one, near, off_oth[0], j_other)
    two_on, two_off = on_swap(two), off_swap(two)
    near = beside(depth_one, depth_two, z_oth[1], on_oth[1])
    three = first(first_product, "first_product", 2, depth_one, depth_two, near, off_oth[1], (*j_own, *j_other))
    three_on, three_off = [on_swap(x) for x in three], [off_swap(x) for x in three]

    own, oth = [], []
    for packed, depth, products in (
        (True, depth_one, (one, one_on, one_off, two, two_on, two_off)),
        (False, depth_two, tuple(x[h] for h in range(2) for x in (three, three_on, three_off))),
    ):
        mine, send = second(packed, depth, products)
        own.append(mine)
        oth.append(across(send))
    return call(
        functools.partial(finish, len(CHUNKS)),
        f32(inverse_blocks.shape),
        "finish",
        scratch=[pltpu.VMEM(inverse_blocks.shape, jnp.float32), pltpu.SemaphoreType.DMA((rows,))],
        specs=[vmem] * (1 + 2 * len(CHUNKS)),
        out_specs=anywhere,
        nbytes=12 << 18,
    )(inverse_blocks, *own, *oth)


def solution(mesh):
    in_specs = (
        P("rows", None, "inner", None),
        P("rows", None, "inner", None),
        P("rows", None),
        P(),
    )
    out_specs = P("rows", None, "inner", None)
    halved = mesh.shape["inner"] == 2 and mesh.shape["rows"] % 2 == 0
    shards = half_shards if halved else general_shards
    return jax.shard_map(shards, mesh=mesh, in_specs=in_specs, out_specs=out_specs, check_vma=False)
```

```python
import functools

import jax
import jax.numpy as jnp
from jax import lax
from jax.experimental import pallas as pl
from jax.experimental.pallas import tpu as pltpu
from jax.sharding import PartitionSpec as P

REACH = 5
CHUNKS = (32, 32)
VMEM_BYTES = 14 * 1024 * 1024


def with_halo(cells, sides, width):
    for axis, dim in sides:
        count = lax.axis_size(axis)
        ends = count - 1
        head = lax.slice_in_dim(cells, 0, width, axis=dim)
        tail = lax.slice_in_dim(cells, cells.shape[dim] - width, cells.shape[dim], axis=dim)
        cells = jnp.concatenate(
            [
                lax.ppermute(tail, axis, [(i, (i + 1) % count) for i in range(ends)]),
                cells,
                lax.ppermute(head, axis, [((i + 1) % count, i) for i in range(ends)]),
            ],
            axis=dim,
        )
    return cells


def match_slots(left_pattern, target_pattern, right_pattern, base):
    local = left_pattern - base
    listed = jnp.take(right_pattern, local, axis=0)
    equal = listed[:, :, None, :] == target_pattern[:, None, :, None]
    width = right_pattern.shape[1]
    slot = jnp.sum(jnp.where(equal, jnp.arange(width, dtype=jnp.int32), 0), axis=3)
    return local[:, :, None], slot, jnp.any(equal, axis=3)


def locate_blocks(left_pattern, target_pattern, right_pattern, base):
    local, slot, found = match_slots(left_pattern, target_pattern, right_pattern, base)
    width = right_pattern.shape[1]
    return jnp.where(found, local * width + slot, right_pattern.shape[0] * width)


def make_fold(left, flat, total, piece):
    count = piece.shape[2]
    lined = piece.reshape(piece.shape[0] * piece.shape[1], count, piece.shape[3])
    lined = jnp.concatenate([lined, jnp.zeros((1, count, piece.shape[3]), lined.dtype)], axis=0)
    for slot in range(flat.shape[1]):
        chosen = jnp.take(lined, flat[:, slot].reshape(-1), axis=0)
        chosen = chosen.reshape(flat.shape[0], flat.shape[2], count, piece.shape[3])
        total = total + jnp.einsum(
            "irp,ikpd->ikrd", left[:, slot], chosen, precision=lax.Precision.HIGHEST
        )
    return total


def patterns_beside(inverse_pattern, count_rows):
    first_row = lax.axis_index("rows") * count_rows
    padded = jnp.pad(inverse_pattern, ((REACH, REACH), (0, 0)), constant_values=-1)
    beside_all = lax.dynamic_slice_in_dim(padded, first_row, count_rows + 2 * REACH, 0)
    own_pattern = lax.dynamic_slice_in_dim(inverse_pattern, first_row, count_rows, 0)
    return first_row - REACH, beside_all, own_pattern


def general_shards(hardness_blocks, inverse_blocks, hardness_pattern, inverse_pattern):
    count_rows = inverse_blocks.shape[0]
    base, beside_all, own_pattern = patterns_beside(inverse_pattern, count_rows)
    flat_one = locate_blocks(hardness_pattern, own_pattern, beside_all, base)
    flat_two = locate_blocks(own_pattern, own_pattern, beside_all, base)
    empty = jnp.zeros(
        (count_rows, own_pattern.shape[1], inverse_blocks.shape[2], inverse_blocks.shape[3]),
        jnp.float32,
    )
    extended = with_halo(inverse_blocks, (("rows", 0),), REACH)
    product = make_fold(
        hardness_blocks, flat_one, empty, lax.all_gather(extended, "inner", axis=2, tiled=True)
    )
    product_ext = with_halo(product, (("rows", 0),), REACH)
    carried = make_fold(
        inverse_blocks, flat_two, empty, lax.all_gather(product_ext, "inner", axis=2, tiled=True)
    )
    return 2.0 * inverse_blocks - carried


def call(body, outs, name, scratch=(), specs=None, out_specs=None, flops=0, nbytes=0):
    params = dict(
        out_shape=outs,
        scratch_shapes=list(scratch),
        compiler_params=pltpu.CompilerParams(vmem_limit_bytes=VMEM_BYTES),
        name=name,
        cost_estimate=pl.CostEstimate(flops=flops, bytes_accessed=nbytes, transcendentals=0),
    )
    if specs is not None:
        params.update(in_specs=specs)
    if out_specs is not None:
        params.update(out_specs=out_specs)
    return pl.pallas_call(body, **params)


def is_low(shape):
    return lax.broadcasted_iota(jnp.int32, shape, len(shape) - 1) < shape[-1] // 2


def swapped(x):
    return pltpu.roll(x, x.shape[-1] // 2, x.ndim - 1)


def unzip_lanes(a, b):
    low = is_low(a.shape)
    return jnp.where(low, a, swapped(b)), jnp.where(low, swapped(a), b)


def halves(x):
    high = x.astype(jnp.bfloat16)
    return high, (x - high.astype(jnp.float32)).astype(jnp.bfloat16)


def find_blocks(left_ref, pattern_ref, one_ref, two_ref, table):
    rows = left_ref.shape[0]
    slots = pattern_ref.shape[1]
    device = lax.axis_index("rows")
    first = device * rows
    last = pattern_ref.shape[0] - 1
    odd = device % 2
    width = 2 * REACH + 1
    none = 3 * rows * slots

    @pl.loop(0, 3 * rows)
    def _(n):
        for shift in range(width):
            table[n * width + shift] = none

    for n, segment in enumerate((2 - odd, 0, 1 + odd)):

        @pl.loop(0, rows)
        def _(r):
            local = n * rows + r
            row = jnp.clip(first + local - rows, 0, last)
            shifts = [pattern_ref[row, k] - row + REACH for k in range(slots)]
            for k, shift in enumerate(shifts):
                table[local * width + shift] = (segment * rows + r) * slots + k

    @pl.loop(0, rows)
    def _(i):
        columns = [pattern_ref[first + i, k] for k in range(slots)]
        for count, lefts, out_ref in (
            (left_ref.shape[1], [left_ref[i, s] for s in range(left_ref.shape[1])], one_ref),
            (slots, columns, two_ref),
        ):
            found = []
            for row in lefts:
                at = (row - first + rows) * width
                for column in columns:
                    shift = column - row + REACH
                    inside = (shift >= 0) & (shift < width)
                    found.append(jnp.where(inside, table[at + jnp.clip(shift, 0, width - 1)], none))
            for n, value in enumerate(found):
                out_ref[i * count * slots + n] = value


def split_columns(send, z_ref, *refs):
    out_refs = refs[0 if send else 1 :]
    second = lax.axis_index("inner") == 1
    rows, slots, half, lanes = z_ref.shape
    for i in range(rows):
        for j in range(slots // 2):
            turned = z_ref[i, 2 * j : 2 * j + 2].reshape(2 * half, lanes).T
            top, bottom = turned[:half], turned[half:]
            part = jnp.where(second, top, bottom) if send else jnp.where(second, bottom, top)
            start = 0
            for out_ref in out_refs:
                depth = out_ref.shape[2]
                out_ref[i, j] = part[start : start + depth]
                start += depth


def gather_dot(index_ref, i, right_slots, out_slots, high_ref, low_ref, lhs_high, lhs_low, right, dims):
    depth = high_ref.shape[1]
    for s in range(right_slots):
        for k in range(out_slots):
            at = index_ref[(i * right_slots + s) * out_slots + k]
            place = (pl.ds(k * depth, depth), pl.ds(s * 128, 128))
            lhs_high[place] = high_ref[at]
            lhs_low[place] = low_ref[at]
    dot = functools.partial(
        lax.dot_general, dimension_numbers=(dims, ((), ())), preferred_element_type=jnp.float32
    )
    both, high = right
    total = dot(lhs_high[...], both)
    count = total.shape[1] // 2
    return total[:, :count] + (total[:, count:] + dot(lhs_low[...], high))


def turn_lanes(x):
    return jnp.where(lax.axis_index("inner") == 1, swapped(x), x)


def left_rows(j_ref, high_ref, low_ref):
    for i in range(j_ref.shape[0]):
        for s in range(j_ref.shape[1]):
            place = (i, slice(None), pl.ds(s * 128, 128))
            high_ref[place], low_ref[place] = halves(turn_lanes(j_ref[i, s]))


def merge_near(start, z_own, z_oth, on_own, on_oth, high_ref, low_ref):
    rows, pairs, depth, lanes = z_oth.shape
    mine = pl.ds(start, depth)
    for g, (own, oth) in enumerate(((z_own, z_oth), (on_own, on_oth))):
        for i in range(rows):
            for j in range(pairs):
                at = ((g * rows + i) * pairs + j) * 2
                even, odd = unzip_lanes(own[i, j, mine], oth[i, j])
                high_ref[at], low_ref[at] = halves(even)
                high_ref[at + 1], low_ref[at + 1] = halves(odd)


def take_blocks(start, near_high, near_low, off_own, off_oth, off_in, z_high, z_low, sem):
    rows, pairs, depth, lanes = off_oth.shape
    near = near_high.shape[0]
    copy = pltpu.make_async_copy(off_own.at[:, :, pl.ds(start, depth)], off_in, sem)
    copy.start()
    z_high[:near], z_low[:near] = near_high[...], near_low[...]
    blank = z_high.shape[0] - 1
    z_high[blank] = jnp.zeros(z_high.shape[1:], jnp.bfloat16)
    z_low[blank] = jnp.zeros(z_low.shape[1:], jnp.bfloat16)
    copy.wait()
    for i in range(rows):
        for j in range(pairs):
            even, odd = unzip_lanes(off_in[i, j], off_oth[i, j])
            at = near + (i * pairs + j) * 2
            z_high[at], z_low[at] = halves(even)
            z_high[at + 1], z_low[at + 1] = halves(odd)


def first_product(start, index_ref, near_high, near_low, off_own, off_oth, j_own_high, j_own_low,
                  j_oth_high, j_oth_low, p_ref, p_rest_ref, off_in, z_high, z_low, j_both, lhs_high, lhs_low,
                  sems):
    rows, pairs, depth, lanes = off_oth.shape
    half, slots = j_own_high.shape[1], j_own_high.shape[2] // 128
    for n, part in enumerate((j_own_high, j_oth_high, j_own_low, j_oth_low)):
        j_both[:, n * half : (n + 1) * half] = part[...]
    take_blocks(start, near_high, near_low, off_own, off_oth, off_in, z_high, z_low, sems.at[0])
    for i in range(rows):
        total = gather_dot(index_ref, i, slots, 2 * pairs, z_high, z_low, lhs_high, lhs_low,
                           (j_both[i], j_both[i, : 2 * half]), ((1,), (1,)))
        total = total.reshape(2 * pairs, depth, lanes)
        p_ref[i], p_rest_ref[i] = total[:pairs], total[pairs:]


def first_half_product(start, index_ref, near_high, near_low, off_own, off_oth, rows_high, rows_low,
                       p_ref, off_in, z_high, z_low, j_both, lhs_high, lhs_low, sems):
    rows, pairs, depth, lanes = off_oth.shape
    half, slots = rows_high.shape[1], rows_high.shape[2] // 128
    for n, part in enumerate((rows_high, rows_high, rows_low, rows_low)):
        j_both[:, n * half : (n + 1) * half] = part[...]
    take_blocks(start, near_high, near_low, off_own, off_oth, off_in, z_high, z_low, sems.at[0])
    for i in range(rows):
        total = gather_dot(index_ref, i, slots, 2 * pairs, z_high, z_low, lhs_high, lhs_low,
                           (j_both[i], j_both[i, : 2 * half]), ((1,), (1,)))
        total = total.reshape(2 * pairs, depth, lanes)
        for j in range(pairs):
            p_ref[i, j] = jnp.where(is_low((depth, lanes)), total[2 * j], total[2 * j + 1])


def left_blocks(chunks, z_own, z_rest, *refs):
    z_send, z_oth, both_ref = refs[:chunks], refs[chunks : 2 * chunks], refs[-1]
    rows, pairs, half, lanes = z_own.shape
    for i in range(rows):
        for j in range(pairs):
            oth = jnp.concatenate([ref[i, j] for ref in z_oth], axis=0)
            send = jnp.concatenate([ref[i, j] for ref in z_send], axis=0)
            for part, (x, y) in enumerate(((z_own[i, j], oth), (send, z_rest[i, j]))):
                for slot, block in enumerate(unzip_lanes(x, y)):
                    place = pl.ds((2 * j + slot) * lanes + part * half, half)
                    both_ref[i, place, :lanes], both_ref[i, place, lanes:] = halves(block)


def second_product(packed, index_ref, *refs):
    sources, (l_both, own_ref, send_ref, p_high, p_low, lhs_high, lhs_low) = refs[:6], refs[6:]
    rows, pairs, depth, lanes = own_ref.shape
    slots = 2 * pairs
    blank = p_high.shape[0] - 1
    p_high[blank] = jnp.zeros(p_high.shape[1:], jnp.bfloat16)
    p_low[blank] = jnp.zeros(p_low.shape[1:], jnp.bfloat16)
    for g in range(3):
        for i in range(rows):
            for j in range(pairs):
                blocks = sources[g][i, j], sources[3 + g][i, j]
                places = j, pairs + j
                if packed:
                    blocks = unzip_lanes(*blocks)
                    places = 2 * j, 2 * j + 1
                for slot, block in zip(places, blocks):
                    at = (g * rows + i) * slots + slot
                    p_high[at], p_low[at] = halves(block)
    for i in range(rows):
        total = gather_dot(index_ref, i, slots, slots, p_high, p_low, lhs_high, lhs_low,
                           (l_both[i], l_both[i, :, :128]), ((1,), (0,)))
        total = total.reshape(slots, depth, lanes)
        for j in range(pairs):
            own_ref[i, j], send_ref[i, j] = unzip_lanes(total[2 * j], total[2 * j + 1])


def left_and_second_product(index_ref, *refs):
    sources, left, rest = refs[:6], refs[6:12], refs[12:]
    own_ref, send_ref, l_both, *scratch = rest
    left_blocks(2, *left, l_both)
    second_product(True, index_ref, *sources, l_both, own_ref, send_ref, *scratch)


def turned_back(start, half, own, oth):
    depth, lanes = own.shape
    parts = []
    for part in (own, oth):
        parts += [jnp.zeros((start, lanes), part.dtype), part]
        parts += [jnp.zeros((half - start - depth, lanes), part.dtype)]
    turned = jnp.concatenate([part for part in parts if part.shape[0]], axis=0).T
    return jnp.where(lax.axis_index("inner") == 1, swapped(turned), turned)


def begin_finish(z_ref, own_ref, oth_ref, out_ref):
    rows, slots, half, lanes = z_ref.shape
    for i in range(rows):
        for j in range(slots // 2):
            turned = turned_back(0, half, own_ref[i, j], oth_ref[i, j])
            pair = slice(2 * j, 2 * j + 2)
            out_ref[i, pair] = 2.0 * z_ref[i, pair] - turned.reshape(2, half, lanes)


def finish(begun_ref, own_ref, oth_ref, out_ref, staged, sems):
    rows, slots, half, lanes = begun_ref.shape
    copies = []
    for i in range(rows):
        for j in range(slots // 2):
            turned = turned_back(half - own_ref.shape[2], half, own_ref[i, j], oth_ref[i, j])
            pair = slice(2 * j, 2 * j + 2)
            staged[i, pair] = begun_ref[i, pair] - turned.reshape(2, half, lanes)
        copies.append(pltpu.make_async_copy(staged.at[i], out_ref.at[i], sems.at[i]))
        copies[-1].start()
    for copy in copies:
        copy.wait()


def half_shards(hardness_blocks, inverse_blocks, hardness_pattern, inverse_pattern):
    rows, slots, half, lanes = inverse_blocks.shape
    left_slots = hardness_blocks.shape[1]
    pairs = slots // 2
    count = lax.axis_size("rows")
    f32 = functools.partial(jax.ShapeDtypeStruct, dtype=jnp.float32)
    bf16 = functools.partial(jax.ShapeDtypeStruct, dtype=jnp.bfloat16)
    pack = f32((rows, pairs, half, lanes))
    smem = pl.BlockSpec(memory_space=pltpu.SMEM)
    vmem = pl.BlockSpec(memory_space=pltpu.VMEM)
    hbm = pl.BlockSpec(memory_space=pltpu.HBM)
    anywhere = pl.BlockSpec(memory_space=pl.ANY)

    def across(x):
        return lax.ppermute(x, "inner", [(0, 1), (1, 0)])

    def on_swap(x):
        return lax.ppermute(x, "rows", [(i, i ^ 1) for i in range(count)])

    def off_swap(x):
        inside = [(i, i + 1) for i in range(1, count - 1, 2)]
        return lax.ppermute(x, "rows", inside + [(b, a) for a, b in inside])

    find = call(
        find_blocks,
        (
            jax.ShapeDtypeStruct((rows * left_slots * slots,), jnp.int32),
            jax.ShapeDtypeStruct((rows * slots * slots,), jnp.int32),
        ),
        "find_blocks",
        scratch=[pltpu.SMEM((3 * rows * (2 * REACH + 1),), jnp.int32)],
        specs=[smem, smem],
        out_specs=[smem, smem],
    )
    take_rows = call(left_rows, (bf16((rows, half, left_slots * lanes)),) * 2, "left_rows")
    chunks = [f32((rows, pairs, depth, lanes)) for depth in CHUNKS]
    z_send = call(functools.partial(split_columns, True), tuple(chunks), "split_send")(inverse_blocks)
    z_own = call(functools.partial(split_columns, False), pack, "split_own", specs=[vmem, anywhere])(
        inverse_blocks, z_send[0]
    )
    z_oth = [across(x) for x in z_send]
    off_own = off_swap(z_own)
    z_send = list(z_send)
    on_own = on_swap(z_own)
    after = lax.optimization_barrier
    inverse_pattern, z_own = after((inverse_pattern, z_own))
    flat_one, flat_two = find(hardness_pattern, inverse_pattern)
    z_oth[1], flat_one = after((z_oth[1], flat_one))
    later, flat_one = after((hardness_blocks, flat_one))
    j_oth = across(later)
    off_oth = [off_swap(x) for x in z_oth]
    on_oth = [on_swap(x) for x in z_oth]
    later, off_own = after((hardness_blocks, off_own))
    j_own = list(take_rows(later))
    blocks = 3 * rows * slots + 1
    bf16_buffer = functools.partial(pltpu.VMEM, dtype=jnp.bfloat16)

    def beside(start, depth, z_oth, on_oth):
        return call(
            functools.partial(merge_near, start), (bf16((2 * rows * slots, depth, lanes)),) * 2, "merge_near"
        )(z_own, z_oth, on_own, on_oth)

    def first(body, name, count, start, depth, near, off_oth, j_rows):
        return call(
            functools.partial(body, start),
            (f32((rows, pairs, depth, lanes)),) * count,
            name,
            scratch=[pltpu.VMEM((rows, pairs, depth, lanes), jnp.float32)]
            + [bf16_buffer((blocks, depth, lanes))] * 2
            + [bf16_buffer((rows, 2 * lanes, left_slots * lanes))]
            + [bf16_buffer((slots * depth, left_slots * lanes))] * 2
            + [pltpu.SemaphoreType.DMA((1,))],
            specs=[smem, vmem, vmem, hbm, vmem] + [vmem] * len(j_rows),
        )(flat_one, *near, off_own, off_oth, *j_rows)

    def second(body, name, depth, operands, *more):
        return call(
            body,
            (f32((rows, pairs, depth, lanes)),) * 2 + more,
            name,
            scratch=[bf16_buffer((blocks, depth, lanes))] * 2
            + [bf16_buffer((slots * depth, slots * lanes))] * 2,
            specs=[smem] + [vmem] * len(operands),
        )(flat_two, *operands)

    depth_one, depth_two = CHUNKS
    z_near, j_own[0] = after((z_oth[0], j_own[0]))
    near = beside(0, depth_one, z_near, on_oth[0])
    later, *near = after((z_own, *near))
    z_rest = across(later)
    (one,) = first(first_half_product, "first_half_product", 1, 0, depth_one, near, off_oth[0], j_own)
    one_on, one_off = on_swap(one), off_swap(one)
    j_other = take_rows(j_oth)
    (two,) = first(first_half_product, "first_half_product", 1, 0, depth_one, near, off_oth[0], j_other)
    two_on, two_off = on_swap(two), off_swap(two)
    near = beside(depth_one, depth_two, z_oth[1], on_oth[1])
    three = first(first_product, "first_product", 2, depth_one, depth_two, near, off_oth[1], (*j_own, *j_other))
    three_on, three_off = [on_swap(x) for x in three], [off_swap(x) for x in three]

    mine_one, send_one, left = second(
        left_and_second_product,
        "left_and_second_product",
        depth_one,
        (one, one_on, one_off, two, two_on, two_off, z_own, z_rest, *z_send, *z_oth),
        bf16((rows, slots * lanes, 2 * lanes)),
    )
    mine_two, send_two = second(
        functools.partial(second_product, False),
        "second_product",
        depth_two,
        (*(x[h] for h in range(2) for x in (three, three_on, three_off)), left),
    )
    begun = call(begin_finish, f32(inverse_blocks.shape), "begin_finish", specs=[vmem] * 3)(
        inverse_blocks, mine_one, across(send_one)
    )
    return call(
        finish,
        f32(inverse_blocks.shape),
        "finish",
        scratch=[pltpu.VMEM(inverse_blocks.shape, jnp.float32), pltpu.SemaphoreType.DMA((rows,))],
        specs=[vmem] * 3,
        out_specs=anywhere,
    )(begun, mine_two, across(send_two))


def solution(mesh):
    in_specs = (
        P("rows", None, "inner", None),
        P("rows", None, "inner", None),
        P("rows", None),
        P(),
    )
    out_specs = P("rows", None, "inner", None)
    halved = mesh.shape["inner"] == 2 and mesh.shape["rows"] % 2 == 0
    shards = half_shards if halved else general_shards
    return jax.shard_map(shards, mesh=mesh, in_specs=in_specs, out_specs=out_specs, check_vma=False)
```

```python
import functools

import jax
import jax.numpy as jnp
from jax import lax
from jax.experimental import pallas as pl
from jax.experimental.pallas import tpu as pltpu
from jax.sharding import PartitionSpec as P

REACH = 5
CHUNKS = (32, 32)
VMEM_BYTES = 14 * 1024 * 1024


def with_halo(cells, sides, width):
    for axis, dim in sides:
        count = lax.axis_size(axis)
        ends = count - 1
        head = lax.slice_in_dim(cells, 0, width, axis=dim)
        tail = lax.slice_in_dim(cells, cells.shape[dim] - width, cells.shape[dim], axis=dim)
        cells = jnp.concatenate(
            [
                lax.ppermute(tail, axis, [(i, (i + 1) % count) for i in range(ends)]),
                cells,
                lax.ppermute(head, axis, [((i + 1) % count, i) for i in range(ends)]),
            ],
            axis=dim,
        )
    return cells


def match_slots(left_pattern, target_pattern, right_pattern, base):
    local = left_pattern - base
    listed = jnp.take(right_pattern, local, axis=0)
    equal = listed[:, :, None, :] == target_pattern[:, None, :, None]
    width = right_pattern.shape[1]
    slot = jnp.sum(jnp.where(equal, jnp.arange(width, dtype=jnp.int32), 0), axis=3)
    return local[:, :, None], slot, jnp.any(equal, axis=3)


def locate_blocks(left_pattern, target_pattern, right_pattern, base):
    local, slot, found = match_slots(left_pattern, target_pattern, right_pattern, base)
    width = right_pattern.shape[1]
    return jnp.where(found, local * width + slot, right_pattern.shape[0] * width)


def make_fold(left, flat, total, piece):
    count = piece.shape[2]
    lined = piece.reshape(piece.shape[0] * piece.shape[1], count, piece.shape[3])
    lined = jnp.concatenate([lined, jnp.zeros((1, count, piece.shape[3]), lined.dtype)], axis=0)
    for slot in range(flat.shape[1]):
        chosen = jnp.take(lined, flat[:, slot].reshape(-1), axis=0)
        chosen = chosen.reshape(flat.shape[0], flat.shape[2], count, piece.shape[3])
        total = total + jnp.einsum(
            "irp,ikpd->ikrd", left[:, slot], chosen, precision=lax.Precision.HIGHEST
        )
    return total


def patterns_beside(inverse_pattern, count_rows):
    first_row = lax.axis_index("rows") * count_rows
    padded = jnp.pad(inverse_pattern, ((REACH, REACH), (0, 0)), constant_values=-1)
    beside_all = lax.dynamic_slice_in_dim(padded, first_row, count_rows + 2 * REACH, 0)
    own_pattern = lax.dynamic_slice_in_dim(inverse_pattern, first_row, count_rows, 0)
    return first_row - REACH, beside_all, own_pattern


def general_shards(hardness_blocks, inverse_blocks, hardness_pattern, inverse_pattern):
    count_rows = inverse_blocks.shape[0]
    base, beside_all, own_pattern = patterns_beside(inverse_pattern, count_rows)
    flat_one = locate_blocks(hardness_pattern, own_pattern, beside_all, base)
    flat_two = locate_blocks(own_pattern, own_pattern, beside_all, base)
    empty = jnp.zeros(
        (count_rows, own_pattern.shape[1], inverse_blocks.shape[2], inverse_blocks.shape[3]),
        jnp.float32,
    )
    extended = with_halo(inverse_blocks, (("rows", 0),), REACH)
    product = make_fold(
        hardness_blocks, flat_one, empty, lax.all_gather(extended, "inner", axis=2, tiled=True)
    )
    product_ext = with_halo(product, (("rows", 0),), REACH)
    carried = make_fold(
        inverse_blocks, flat_two, empty, lax.all_gather(product_ext, "inner", axis=2, tiled=True)
    )
    return 2.0 * inverse_blocks - carried


def call(body, outs, name, scratch=(), specs=None, out_specs=None, flops=0, nbytes=0):
    params = dict(
        out_shape=outs,
        scratch_shapes=list(scratch),
        compiler_params=pltpu.CompilerParams(vmem_limit_bytes=VMEM_BYTES),
        name=name,
        cost_estimate=pl.CostEstimate(flops=flops, bytes_accessed=nbytes, transcendentals=0),
    )
    if specs is not None:
        params.update(in_specs=specs)
    if out_specs is not None:
        params.update(out_specs=out_specs)
    return pl.pallas_call(body, **params)


def is_low(shape):
    return lax.broadcasted_iota(jnp.int32, shape, len(shape) - 1) < shape[-1] // 2


def swapped(x):
    return pltpu.roll(x, x.shape[-1] // 2, x.ndim - 1)


def unzip_lanes(a, b):
    low = is_low(a.shape)
    return jnp.where(low, a, swapped(b)), jnp.where(low, swapped(a), b)


def halves(x):
    high = x.astype(jnp.bfloat16)
    return high, (x - high.astype(jnp.float32)).astype(jnp.bfloat16)


def find_blocks(left_ref, pattern_ref, one_ref, two_ref, table):
    rows = left_ref.shape[0]
    slots = pattern_ref.shape[1]
    device = lax.axis_index("rows")
    first = device * rows
    last = pattern_ref.shape[0] - 1
    odd = device % 2
    width = 2 * REACH + 1
    none = 3 * rows * slots

    @pl.loop(0, 3 * rows)
    def _(n):
        for shift in range(width):
            table[n * width + shift] = none

    for n, segment in enumerate((2 - odd, 0, 1 + odd)):

        @pl.loop(0, rows)
        def _(r):
            local = n * rows + r
            row = jnp.clip(first + local - rows, 0, last)
            shifts = [pattern_ref[row, k] - row + REACH for k in range(slots)]
            for k, shift in enumerate(shifts):
                table[local * width + shift] = (segment * rows + r) * slots + k

    @pl.loop(0, rows)
    def _(i):
        columns = [pattern_ref[first + i, k] for k in range(slots)]
        for count, lefts, out_ref in (
            (left_ref.shape[1], [left_ref[i, s] for s in range(left_ref.shape[1])], one_ref),
            (slots, columns, two_ref),
        ):
            found = []
            for row in lefts:
                at = (row - first + rows) * width
                for column in columns:
                    shift = column - row + REACH
                    inside = (shift >= 0) & (shift < width)
                    found.append(jnp.where(inside, table[at + jnp.clip(shift, 0, width - 1)], none))
            for n, value in enumerate(found):
                out_ref[i * count * slots + n] = value


def split_columns(send, z_ref, *refs):
    out_refs = refs[0 if send else 1 :]
    second = lax.axis_index("inner") == 1
    rows, slots, half, lanes = z_ref.shape
    for i in range(rows):
        for j in range(slots // 2):
            turned = z_ref[i, 2 * j : 2 * j + 2].reshape(2 * half, lanes).T
            top, bottom = turned[:half], turned[half:]
            part = jnp.where(second, top, bottom) if send else jnp.where(second, bottom, top)
            start = 0
            for out_ref in out_refs:
                depth = out_ref.shape[2]
                out_ref[i, j] = part[start : start + depth]
                start += depth


def gather_dot(index_ref, i, right_slots, out_slots, high_ref, low_ref, lhs_high, lhs_low, right, dims):
    depth = high_ref.shape[1]
    for s in range(right_slots):
        for k in range(out_slots):
            at = index_ref[(i * right_slots + s) * out_slots + k]
            place = (pl.ds(k * depth, depth), pl.ds(s * 128, 128))
            lhs_high[place] = high_ref[at]
            lhs_low[place] = low_ref[at]
    dot = functools.partial(
        lax.dot_general, dimension_numbers=(dims, ((), ())), preferred_element_type=jnp.float32
    )
    both, high = right
    total = dot(lhs_high[...], both)
    count = total.shape[1] // 2
    return total[:, :count] + (total[:, count:] + dot(lhs_low[...], high))


def turn_lanes(x):
    return jnp.where(lax.axis_index("inner") == 1, swapped(x), x)


def left_rows(j_ref, high_ref, low_ref):
    for i in range(j_ref.shape[0]):
        for s in range(j_ref.shape[1]):
            place = (i, slice(None), pl.ds(s * 128, 128))
            high_ref[place], low_ref[place] = halves(turn_lanes(j_ref[i, s]))


def merge_near(start, z_own, z_oth, on_own, on_oth, high_ref, low_ref):
    rows, pairs, depth, lanes = z_oth.shape
    mine = pl.ds(start, depth)
    for g, (own, oth) in enumerate(((z_own, z_oth), (on_own, on_oth))):
        for i in range(rows):
            for j in range(pairs):
                at = ((g * rows + i) * pairs + j) * 2
                even, odd = unzip_lanes(own[i, j, mine], oth[i, j])
                high_ref[at], low_ref[at] = halves(even)
                high_ref[at + 1], low_ref[at + 1] = halves(odd)


def take_blocks(start, near_high, near_low, off_own, off_oth, off_in, z_high, z_low, sem):
    rows, pairs, depth, lanes = off_oth.shape
    near = near_high.shape[0]
    copy = pltpu.make_async_copy(off_own.at[:, :, pl.ds(start, depth)], off_in, sem)
    copy.start()
    z_high[:near], z_low[:near] = near_high[...], near_low[...]
    blank = z_high.shape[0] - 1
    z_high[blank] = jnp.zeros(z_high.shape[1:], jnp.bfloat16)
    z_low[blank] = jnp.zeros(z_low.shape[1:], jnp.bfloat16)
    copy.wait()
    for i in range(rows):
        for j in range(pairs):
            even, odd = unzip_lanes(off_in[i, j], off_oth[i, j])
            at = near + (i * pairs + j) * 2
            z_high[at], z_low[at] = halves(even)
            z_high[at + 1], z_low[at + 1] = halves(odd)


def first_product(start, index_ref, near_high, near_low, off_own, off_oth, j_own_high, j_own_low,
                  j_oth_high, j_oth_low, p_ref, p_rest_ref, off_in, z_high, z_low, j_both, lhs_high, lhs_low,
                  sems):
    rows, pairs, depth, lanes = off_oth.shape
    half, slots = j_own_high.shape[1], j_own_high.shape[2] // 128
    for n, part in enumerate((j_own_high, j_oth_high, j_own_low, j_oth_low)):
        j_both[:, n * half : (n + 1) * half] = part[...]
    take_blocks(start, near_high, near_low, off_own, off_oth, off_in, z_high, z_low, sems.at[0])
    for i in range(rows):
        total = gather_dot(index_ref, i, slots, 2 * pairs, z_high, z_low, lhs_high, lhs_low,
                           (j_both[i], j_both[i, : 2 * half]), ((1,), (1,)))
        total = total.reshape(2 * pairs, depth, lanes)
        part = p_ref.shape[2]
        p_ref[i], p_rest_ref[i] = total[:, :part], total[:, part:]


def first_half_product(start, index_ref, near_high, near_low, off_own, off_oth, rows_high, rows_low,
                       p_ref, off_in, z_high, z_low, j_both, lhs_high, lhs_low, sems):
    rows, pairs, depth, lanes = off_oth.shape
    half, slots = rows_high.shape[1], rows_high.shape[2] // 128
    for n, part in enumerate((rows_high, rows_high, rows_low, rows_low)):
        j_both[:, n * half : (n + 1) * half] = part[...]
    take_blocks(start, near_high, near_low, off_own, off_oth, off_in, z_high, z_low, sems.at[0])
    for i in range(rows):
        total = gather_dot(index_ref, i, slots, 2 * pairs, z_high, z_low, lhs_high, lhs_low,
                           (j_both[i], j_both[i, : 2 * half]), ((1,), (1,)))
        total = total.reshape(2 * pairs, depth, lanes)
        for j in range(pairs):
            p_ref[i, j] = jnp.where(is_low((depth, lanes)), total[2 * j], total[2 * j + 1])


def left_blocks(chunks, z_own, z_rest, *refs):
    z_send, z_oth, both_ref = refs[:chunks], refs[chunks : 2 * chunks], refs[-1]
    rows, pairs, half, lanes = z_own.shape
    for i in range(rows):
        for j in range(pairs):
            oth = jnp.concatenate([ref[i, j] for ref in z_oth], axis=0)
            send = jnp.concatenate([ref[i, j] for ref in z_send], axis=0)
            for part, (x, y) in enumerate(((z_own[i, j], oth), (send, z_rest[i, j]))):
                for slot, block in enumerate(unzip_lanes(x, y)):
                    place = pl.ds((2 * j + slot) * lanes + part * half, half)
                    both_ref[i, place, :lanes], both_ref[i, place, lanes:] = halves(block)


def second_product(packed, index_ref, *refs):
    count = 6 if packed else 3
    sources, (l_both, own_ref, send_ref, p_high, p_low, lhs_high, lhs_low) = refs[:count], refs[count:]
    rows, pairs, depth, lanes = own_ref.shape
    slots = 2 * pairs
    blank = p_high.shape[0] - 1
    p_high[blank] = jnp.zeros(p_high.shape[1:], jnp.bfloat16)
    p_low[blank] = jnp.zeros(p_low.shape[1:], jnp.bfloat16)
    for g in range(3):
        for i in range(rows):
            for j in range(pairs):
                at = (0, 2, 1)[g]
                if packed:
                    blocks = unzip_lanes(sources[at][i, j], sources[3 + g][i, j])
                else:
                    blocks = sources[at][i, 2 * j], sources[at][i, 2 * j + 1]
                for slot, block in enumerate(blocks):
                    at = (g * rows + i) * slots + 2 * j + slot
                    p_high[at], p_low[at] = halves(block)
    for i in range(rows):
        total = gather_dot(index_ref, i, slots, slots, p_high, p_low, lhs_high, lhs_low,
                           (l_both[i], l_both[i, :, :128]), ((1,), (0,)))
        total = total.reshape(slots, depth, lanes)
        for j in range(pairs):
            own_ref[i, j], send_ref[i, j] = unzip_lanes(total[2 * j], total[2 * j + 1])


def left_and_second_product(index_ref, *refs):
    sources, left, rest = refs[:6], refs[6:12], refs[12:]
    own_ref, send_ref, l_both, *scratch = rest
    left_blocks(2, *left, l_both)
    second_product(True, index_ref, *sources, l_both, own_ref, send_ref, *scratch)


def turned_back(start, half, own, oth):
    depth, lanes = own.shape
    parts = []
    for part in (own, oth):
        parts += [jnp.zeros((start, lanes), part.dtype), part]
        parts += [jnp.zeros((half - start - depth, lanes), part.dtype)]
    turned = jnp.concatenate([part for part in parts if part.shape[0]], axis=0).T
    return jnp.where(lax.axis_index("inner") == 1, swapped(turned), turned)


def begin_finish(z_ref, own_ref, oth_ref, out_ref):
    rows, slots, half, lanes = z_ref.shape
    for i in range(rows):
        for j in range(slots // 2):
            turned = turned_back(0, half, own_ref[i, j], oth_ref[i, j])
            pair = slice(2 * j, 2 * j + 2)
            out_ref[i, pair] = 2.0 * z_ref[i, pair] - turned.reshape(2, half, lanes)


def finish(begun_ref, own_one, own_two, oth_one, oth_two, out_ref, staged, sems):
    rows, slots, half, lanes = begun_ref.shape
    copies = []
    for i in range(rows):
        for j in range(slots // 2):
            own = jnp.concatenate([own_one[i, j], own_two[i, j]], axis=0)
            oth = jnp.concatenate([oth_one[i, j], oth_two[i, j]], axis=0)
            turned = turned_back(half - own.shape[0], half, own, oth)
            pair = slice(2 * j, 2 * j + 2)
            staged[i, pair] = begun_ref[i, pair] - turned.reshape(2, half, lanes)
        copies.append(pltpu.make_async_copy(staged.at[i], out_ref.at[i], sems.at[i]))
        copies[-1].start()
    for copy in copies:
        copy.wait()


def half_shards(hardness_blocks, inverse_blocks, hardness_pattern, inverse_pattern):
    rows, slots, half, lanes = inverse_blocks.shape
    left_slots = hardness_blocks.shape[1]
    pairs = slots // 2
    count = lax.axis_size("rows")
    f32 = functools.partial(jax.ShapeDtypeStruct, dtype=jnp.float32)
    bf16 = functools.partial(jax.ShapeDtypeStruct, dtype=jnp.bfloat16)
    pack = f32((rows, pairs, half, lanes))
    smem = pl.BlockSpec(memory_space=pltpu.SMEM)
    vmem = pl.BlockSpec(memory_space=pltpu.VMEM)
    hbm = pl.BlockSpec(memory_space=pltpu.HBM)
    anywhere = pl.BlockSpec(memory_space=pl.ANY)

    def across(x):
        return lax.ppermute(x, "inner", [(0, 1), (1, 0)])

    def on_swap(x):
        return lax.ppermute(x, "rows", [(i, i ^ 1) for i in range(count)])

    def off_swap(x):
        inside = [(i, i + 1) for i in range(1, count - 1, 2)]
        return lax.ppermute(x, "rows", inside + [(b, a) for a, b in inside])

    find = call(
        find_blocks,
        (
            jax.ShapeDtypeStruct((rows * left_slots * slots,), jnp.int32),
            jax.ShapeDtypeStruct((rows * slots * slots,), jnp.int32),
        ),
        "find_blocks",
        scratch=[pltpu.SMEM((3 * rows * (2 * REACH + 1),), jnp.int32)],
        specs=[smem, smem],
        out_specs=[smem, smem],
    )
    take_rows = call(left_rows, (bf16((rows, half, left_slots * lanes)),) * 2, "left_rows")
    chunks = [f32((rows, pairs, depth, lanes)) for depth in CHUNKS]
    z_send = call(functools.partial(split_columns, True), tuple(chunks), "split_send")(inverse_blocks)
    z_own = call(functools.partial(split_columns, False), pack, "split_own", specs=[vmem, anywhere])(
        inverse_blocks, z_send[0]
    )
    z_oth = [across(x) for x in z_send]
    off_own = off_swap(z_own)
    z_send = list(z_send)
    after = lax.optimization_barrier
    inverse_pattern, z_own = after((inverse_pattern, z_own))
    flat_one, flat_two = find(hardness_pattern, inverse_pattern)
    later, flat_one = after((z_own, flat_one))
    on_own = on_swap(later)
    z_oth[1], flat_one = after((z_oth[1], flat_one))
    later, flat_one = after((hardness_blocks, flat_one))
    j_oth = across(later)
    off_oth = [off_swap(x) for x in z_oth]
    on_oth = [on_swap(x) for x in z_oth]
    later, off_own = after((hardness_blocks, off_own))
    j_own = list(take_rows(later))
    blocks = 3 * rows * slots + 1
    bf16_buffer = functools.partial(pltpu.VMEM, dtype=jnp.bfloat16)

    def beside(start, depth, z_oth, on_oth):
        return call(
            functools.partial(merge_near, start), (bf16((2 * rows * slots, depth, lanes)),) * 2, "merge_near"
        )(z_own, z_oth, on_own, on_oth)

    def first(body, name, shapes, start, depth, near, off_oth, j_rows):
        return call(
            functools.partial(body, start),
            shapes,
            name,
            scratch=[pltpu.VMEM((rows, pairs, depth, lanes), jnp.float32)]
            + [bf16_buffer((blocks, depth, lanes))] * 2
            + [bf16_buffer((rows, 2 * lanes, left_slots * lanes))]
            + [bf16_buffer((slots * depth, left_slots * lanes))] * 2
            + [pltpu.SemaphoreType.DMA((1,))],
            specs=[smem, vmem, vmem, hbm, vmem] + [vmem] * len(j_rows),
        )(flat_one, *near, off_own, off_oth, *j_rows)

    def second(body, name, depth, operands, *more):
        return call(
            body,
            (f32((rows, pairs, depth, lanes)),) * 2 + more,
            name,
            scratch=[bf16_buffer((blocks, depth, lanes))] * 2
            + [bf16_buffer((slots * depth, slots * lanes))] * 2,
            specs=[smem] + [vmem] * len(operands),
        )(flat_two, *operands)

    depth_one, depth_two = CHUNKS
    z_near, j_own[0] = after((z_oth[0], j_own[0]))
    near = beside(0, depth_one, z_near, on_oth[0])
    later, *near = after((z_own, *near))
    z_rest = across(later)
    packs = (f32((rows, pairs, depth_one, lanes)),)
    (one,) = first(first_half_product, "first_half_product", packs, 0, depth_one, near, off_oth[0], j_own)
    one_on, one_off = on_swap(one), off_swap(one)
    j_other = take_rows(j_oth)
    (two,) = first(first_half_product, "first_half_product", packs, 0, depth_one, near, off_oth[0], j_other)
    two_on, two_off = on_swap(two), off_swap(two)
    near = beside(depth_one, depth_two, z_oth[1], on_oth[1])
    parts = (f32((rows, slots, depth_two // 2, lanes)),) * 2
    three = first(first_product, "first_product", parts, depth_one, depth_two, near, off_oth[1], (*j_own, *j_other))
    three_on, three_off = [on_swap(x) for x in three], [off_swap(x) for x in three]

    mine_one, send_one, left = second(
        left_and_second_product,
        "left_and_second_product",
        depth_one,
        (one, one_off, one_on, two, two_on, two_off, z_own, z_rest, *z_send, *z_oth),
        bf16((rows, slots * lanes, 2 * lanes)),
    )
    mine_two, oth_two = [], []
    for operands in zip(three, three_off, three_on):
        mine, send = second(
            functools.partial(second_product, False), "second_product", depth_two // 2, (*operands, left)
        )
        mine_two.append(mine)
        oth_two.append(across(send))
    begun = call(begin_finish, f32(inverse_blocks.shape), "begin_finish", specs=[vmem] * 3)(
        inverse_blocks, mine_one, across(send_one)
    )
    return call(
        finish,
        f32(inverse_blocks.shape),
        "finish",
        scratch=[pltpu.VMEM(inverse_blocks.shape, jnp.float32), pltpu.SemaphoreType.DMA((rows,))],
        specs=[vmem] * 5,
        out_specs=anywhere,
    )(begun, *mine_two, *oth_two)


def solution(mesh):
    in_specs = (
        P("rows", None, "inner", None),
        P("rows", None, "inner", None),
        P("rows", None),
        P(),
    )
    out_specs = P("rows", None, "inner", None)
    halved = mesh.shape["inner"] == 2 and mesh.shape["rows"] % 2 == 0
    shards = half_shards if halved else general_shards
    return jax.shard_map(shards, mesh=mesh, in_specs=in_specs, out_specs=out_specs, check_vma=False)
```
